256 devices in a mesh: row: 8 (over y_lo, x), col: 32 (over y_hi, z, core).
Axes of the slice: x: 4, y: 4 (y_hi: 2, y_lo: 2; y = y_hi * 2 + y_lo), z: 8, core: 2. Of those that a mesh axis runs over, the one named last changes fastest.
Arguments:
- ampl: bfloat16 [1792, 256, 1792], P('col', 'row'), may hold values from -0.015625 to 0.015625
- integrals: bfloat16 [1024, 256, 1792], P('col', 'row'), may hold values from -6 to 6
- residual_in: float32 [1792, 1024], P('row', 'col'), may hold values from -6 to 6
- vir_energy: float32 [1792], P('row'), may hold values from 0.2 to 2
- slab_energy: float32 [128], replicated, may hold values from 0.2 to 2
- pair_energy: float32 [8], replicated, may hold values from -1 to -0.3
Outputs:
- update: float32 [1792, 1024], P('row', 'col')
The draws below stay inside these ranges and needn't reach their ends.
All inputs are finite; a program needn't handle non-finite values.
Results may differ from the reference program's by a relative error of at most 0.0003.
Values may be sent and summed in bfloat16 or wider, within the bound.
A program may use at most 64 MiB of HBM per device.

```python
import math
import jax
import jax.numpy as jnp
from jax import lax

OCC = 256
VIR = 1792
SLAB = 128
JWIN = 8
COLS = 1024


def spiked(result, key, source, target, parts, factor):
    def block_of(axis_at):
        return (jnp.arange(result.shape[axis_at]) // (result.shape[axis_at] // parts)).reshape((-1,) + (1,) * (result.ndim - 1 - axis_at))

    first = jax.random.permutation(key, parts)[block_of(target)]
    second = (block_of(target) + parts // 2) % parts
    return jnp.where((block_of(source) == first) | (block_of(source) == second), factor * result, result)


def block_scale(stream_key, dims, shards, least, top_value):
    factor_of, own = 1.0, jax.random.fold_in(stream_key, 6)
    for dim, blocks in shards:
        steps = jnp.exp(jax.random.uniform(jax.random.fold_in(own, dim), (blocks,), jnp.float32, least / len(shards), top_value / len(shards)))
        factor_of = factor_of * jnp.repeat(steps, dims[dim] // blocks).reshape([-1 if axis == dim else 1 for axis in range(len(dims))])
    return factor_of


def bell_draw(rng, dims, deviation, reach, cuts=(), dtype=jnp.bfloat16):
    entries = jax.random.normal(rng, dims, jnp.float32) * deviation
    if len(cuts) > 0:
        entries = block_scale(rng, dims, cuts, -0.22, 0.18) * entries
    return jnp.clip(entries, min=-reach, max=reach).astype(dtype)


def bell_draw_with(own_key, dims, spread, most, split, heavy, kind=jnp.bfloat16):
    values = spread * jax.random.normal(own_key, dims, jnp.float32)
    if split:
        values = values * block_scale(own_key, dims, split, -0.22, 0.18)
    return jnp.clip(spiked(values, jax.random.fold_in(own_key, 3), *heavy), -most, most).astype(kind)


def setup_inputs(seed: int = 0) -> dict:
    arg_keys = jax.random.split(jax.random.key(seed), 7)
    return {
        "ampl": bell_draw_with(arg_keys[0], (VIR, OCC, VIR), (OCC * VIR) ** -0.5, 0.015625, ((0, 32), (1, 8)), (1, 0, 32, 2.75)),
        "integrals": bell_draw_with(arg_keys[1], (COLS, OCC, VIR), 1.0, 6.0, ((0, 32), (1, 8)), (2, 0, 32, 2.75)),
        "residual_in": bell_draw(arg_keys[2], (VIR, COLS), 1.0, 6.0, ((0, 8), (1, 32)), jnp.float32),
        "vir_energy": jnp.clip(jnp.exp(math.log(2.0) - 2.3025851 * jax.random.uniform(arg_keys[3], (VIR,), jnp.float32) ** block_scale(arg_keys[3], (VIR,), ((0, 8),), -0.2, 0.2)), 0.2, 2.0),
        "slab_energy": jnp.clip(jnp.exp(jax.random.uniform(arg_keys[4], (SLAB,), jnp.float32, math.log(0.2), math.log(2.0))), 0.2, 2.0),
        "pair_energy": jnp.clip(jax.random.uniform(arg_keys[5], (JWIN,), jnp.float32, -1.0, -0.3), -1.0, -0.3),
    }


def reference(ampl, integrals, residual_in, vir_energy, slab_energy, pair_energy):
    def add_orbital(total, pieces):
        left, right = pieces
        return total + jnp.dot(left, right.T, preferred_element_type=jnp.float32), None

    start = jnp.zeros((ampl.shape[0], integrals.shape[0]), jnp.float32)
    cycle, unused = lax.scan(add_orbital, start, (jnp.moveaxis(ampl, 1, 0), jnp.moveaxis(integrals, 1, 0)))
    shifted = (slab_energy[None, :] - pair_energy[:, None]).reshape(-1)
    denom = vir_energy[:, None] + shifted[None, :]
    return (residual_in + cycle) / denom
```

```python
import functools

import jax
import jax.numpy as jnp
from jax import lax
from jax.experimental import pallas as pl
from jax.experimental.pallas import tpu as pltpu
from jax.sharding import PartitionSpec as P

SLAB = 128
JWIN = 8
MESH = pl.DeviceIdType.MESH
BF = jnp.bfloat16
F32 = jnp.float32
NX, NY, NZ, NC = 4, 4, 8, 2
ZC = NZ * NC
C = 1792
A_CHUNKS = ((0, 16), (16, 16), (32, 16), (48, 8))
W_CHUNKS = ((0, 16), (16, 16))


def device(x, y, z, c):
    return ((y % 2) * NX + x, ((y // 2) * NZ + z) * NC + c)


def far_first(j):
    return jnp.where(j == NZ - 1, 0, jnp.where(j % 2 == 1, 4 - (j + 1) // 2, 4 + j // 2))


def permutation(rows):
    n = rows * 16
    out = lax.broadcasted_iota(jnp.int32, (n, n), 0)
    inp = lax.broadcasted_iota(jnp.int32, (n, n), 1)
    hit = (out // rows == inp % 16) & (out % rows == inp // 16)
    return jnp.where(hit, 1.0, 0.0).astype(BF)


def kernel(ampl, integ, out0, xbuf, x3buf, perm, perm3, sw, sa, sa3, yw, ya, ya3, rw, ra, ra3,
           half, own, r1, xr, ub, yr, zb, zr,
           load_sem, ys, yrv, zs, zrv, loc_sem, s0s, s0r, s1s, s1r, s2s, s2r, s3s, s3r):
    row = lax.axis_index("row")
    col = lax.axis_index("col")
    ylo, x = row // NX, row % NX
    yhi, z, c = col // ZC, (col // NC) % NZ, col % NC
    y = yhi * 2 + ylo
    zc = z * NC + c

    chunks = [(integ, s, n, sw.at[i], yw.at[i]) for i, (s, n) in enumerate(W_CHUNKS)]
    chunks += [(ampl, s, n, sa.at[i], ya.at[i]) for i, (s, n) in enumerate(A_CHUNKS[:-1])]
    chunks += [(ampl, *A_CHUNKS[-1], sa3, ya3)]
    nw, na = len(W_CHUNKS), len(A_CHUNKS)

    def load(i):
        src, start, rows, _, _ = chunks[i]
        dst = xbuf.at[i % 2] if rows == 16 else x3buf
        return pltpu.make_async_copy(src.at[pl.ds(start, rows)], dst, load_sem.at[i % 2])

    def relayout(i, h):
        _, _, rows, send, _ = chunks[i]

        @pl.loop(0, C // 256)
        def _(j):
            lanes = pl.ds(pl.multiple_of(j * 256, 256), 256)
            if rows == 16:
                block = xbuf[i % 2, :, 16 * h:16 * h + 16, lanes].reshape(256, 256)
                moved = jnp.dot(perm[...], block, preferred_element_type=F32)
                send[16 * h:16 * h + 16, :, lanes] = moved.astype(BF).reshape(16, 16, 256)
            else:
                block = x3buf[:, 16 * h:16 * h + 16, lanes].reshape(128, 256)
                moved = jnp.dot(perm3[...], block, preferred_element_type=F32)
                send[16 * h:16 * h + 16, :, lanes] = moved.reshape(16, rows, 256).astype(BF)

    def y_copy(i, h, zd):
        _, _, _, send, recv = chunks[i]
        return pltpu.make_async_remote_copy(
            src_ref=send.at[pl.ds(h * ZC + zd * NC, NC)],
            dst_ref=recv.at[yhi, pl.ds(zd * NC, NC)],
            send_sem=ys.at[i, h, zd],
            recv_sem=yrv.at[i, yhi, zd],
            device_id=device(x, h * 2 + 1 - ylo, z, c),
            device_id_type=MESH,
        )

    def y_arrived(i, h, zd):
        _, _, _, send, recv = chunks[i]
        return pltpu.make_async_copy(
            send.at[pl.ds(h * ZC + zd * NC, NC)], recv.at[h, pl.ds(zd * NC, NC)], yrv.at[i, h, zd])

    def slot(i, zz, cc):
        if i < nw:
            return rw.at[cc, :, zz, pl.ds(W_CHUNKS[i][0], 16)]
        xa, q = zz // 2, (zz % 2) * 2 + cc
        if i < nw + na - 1:
            return ra.at[i - nw, xa, :, q]
        return ra3.at[xa, :, q]

    def z_copy(i, zd, cd):
        recv = chunks[i][4]
        kk = zd * NC + cd
        return pltpu.make_async_remote_copy(
            src_ref=recv.at[:, kk],
            dst_ref=slot(i, z, c),
            send_sem=zs.at[i, kk],
            recv_sem=zrv.at[i, zc],
            device_id=device(x, y, zd, cd),
            device_id_type=MESH,
        )

    def z_arrived(i, zz, cc):
        recv = chunks[i][4]
        return pltpu.make_async_copy(recv.at[:, zz * NC + cc], slot(i, zz, cc), zrv.at[i, zz * NC + cc])

    def own_copy(i):
        return pltpu.make_async_copy(chunks[i][4].at[:, zc], slot(i, z, c), loc_sem.at[i])

    def prepare(i):
        load(i).wait()
        for h in range(2):
            relayout(i, h)
            if i == 0 and h == 0:
                meet()

            @pl.loop(0, NZ)
            def _(j):
                y_copy(i, h, (z + far_first(j)) % NZ).start()

        if i + 2 < nw + na:
            load(i + 2).start()

    def forward(i):
        @pl.loop(0, NZ - 1)
        def _(j):
            zd = (z + far_first(j)) % NZ
            for h in range(2):
                y_arrived(i, h, zd).wait()
            for cd in range(NC):
                z_copy(i, zd, cd).start()

        for h in range(2):
            y_arrived(i, h, z).wait()
        z_copy(i, z, 1 - c).start()
        own_copy(i).start()

    def sent(i):
        @pl.loop(0, NZ - 1)
        def _(j):
            zd = (z + far_first(j)) % NZ
            for cd in range(NC):
                z_copy(i, zd, cd).wait_send()

        z_copy(i, z, 1 - c).wait_send()

    def arrived(i):
        @pl.loop(0, NZ - 1)
        def _(j):
            zz = (z + far_first(j)) % NZ
            for cc in range(NC):
                z_arrived(i, zz, cc).wait()

        z_arrived(i, z, 1 - c).wait()
        own_copy(i).wait()

    def meet():
        barrier = pltpu.get_barrier_semaphore()
        for d in range(1, NY):
            pl.semaphore_signal(barrier, inc=1, device_id=device(x, (y + d) % NY, z, c), device_id_type=MESH)
        for d in range(1, NX):
            pl.semaphore_signal(barrier, inc=1, device_id=device((x + d) % NX, y, z, c), device_id_type=MESH)
        for d in range(1, NZ):
            for cd in range(NC):
                pl.semaphore_signal(barrier, inc=1, device_id=device(x, y, (z + d) % NZ, cd), device_id_type=MESH)
        pl.semaphore_signal(barrier, inc=1, device_id=device(x, y, z, 1 - c), device_id_type=MESH)
        pl.semaphore_wait(barrier, NY - 1 + NX - 1 + (NZ - 1) * NC + 1)

    contract = (((1,), (1,)), ((), ()))

    def multiply(m, cn, dst):
        rows = A_CHUNKS[m][1]

        @pl.loop(0, 2)
        def _(h):
            right = rw[cn, h].reshape(256, C)
            for xa in range(NX):
                if rows == 16:
                    left = ra[m, xa].reshape(128, C)
                else:
                    left = ra3[xa].astype(F32).reshape(rows * 8, C).astype(BF)
                dst[xa, :, h, :rows * 4, :] = lax.dot_general(
                    left, right, contract, preferred_element_type=F32).reshape(2, rows * 4, 256)

    def half_copy(m):
        n = A_CHUNKS[m][1] * 4
        return pltpu.make_async_remote_copy(
            src_ref=half.at[:, :, :, pl.ds(0, n)], dst_ref=r1.at[m, :, :, :, pl.ds(0, n)],
            send_sem=s0s.at[m], recv_sem=s0r.at[m],
            device_id=device(x, y, z, 1 - c), device_id_type=MESH)

    def x_copy(m, d):
        n = A_CHUNKS[m][1] * 4
        xd = (x + d) % NX
        return pltpu.make_async_remote_copy(
            src_ref=r1.at[m, xd, :, :, pl.ds(0, n)], dst_ref=xr.at[m, d - 1, :, :, pl.ds(0, n)],
            send_sem=s1s.at[m, d - 1], recv_sem=s1r.at[m, d - 1],
            device_id=device(xd, y, z, c), device_id_type=MESH)

    def yr_copy(m, d):
        n = A_CHUNKS[m][1] * 4
        yd = (y + d) % NY
        return pltpu.make_async_remote_copy(
            src_ref=ub.at[m, yd % 2, yd // 2, pl.ds(0, n)], dst_ref=yr.at[m, d - 1, pl.ds(0, n)],
            send_sem=s2s.at[m, d - 1], recv_sem=s2r.at[m, d - 1],
            device_id=device(x, yd, z, c), device_id_type=MESH)

    def zr_copy(m, d):
        zd = (z + d) % NZ
        return pltpu.make_async_remote_copy(
            src_ref=zb.at[m, zd], dst_ref=zr.at[m, d - 1],
            send_sem=s3s.at[m, d - 1], recv_sem=s3r.at[m, d - 1],
            device_id=device(x, y, zd, c), device_id_type=MESH)

    def reduce(m):
        n = A_CHUNKS[m][1] * 4
        if m > 0:
            half_copy(m - 1).wait_send()
        multiply(m, 1 - c, half)
        half_copy(m).start()
        multiply(m, c, own)
        half_copy(m).wait_recv()
        for d in (2, 1, 3, 0):
            xd = (x + d) % NX
            r1[m, xd, :, :, :n] = r1[m, xd, :, :, :n] + own[xd, :, :, :n]
            if d > 0:
                x_copy(m, d).start()
        for d in (1, 3, 2):
            x_copy(m, d).wait_recv()
        ub[m, :, :, :n] = (r1[m, x, :, :, :n] + xr[m, 0, :, :, :n]) + (xr[m, 1, :, :, :n] + xr[m, 2, :, :, :n])
        for d in (2, 1, 3):
            yr_copy(m, d).start()
        for d in (1, 3, 2):
            yr_copy(m, d).wait_recv()
        total = (ub[m, ylo, yhi, :n] + yr[m, 0, :n]) + (yr[m, 1, :n] + yr[m, 2, :n])
        if n < 64:
            total = jnp.concatenate([total, jnp.zeros_like(total)], axis=0)
        total = jnp.concatenate([total, jnp.zeros_like(total)], axis=0)
        zb[m] = total.T.reshape(NZ, 32, 128)
        for d in (4, 3, 5, 2, 6, 1, 7):
            zr_copy(m, d).start()
        for d in range(1, NZ):
            zr_copy(m, d).wait_recv()
        final = zb[m, z] + zr[m, 0]
        for d in range(2, NZ):
            final = final + zr[m, d - 1]
        out0[m] = final

    load(0).start()
    load(1).start()
    perm[...] = permutation(16)
    perm3[...] = permutation(8)

    total = nw + na
    prepare(0)
    prepare(1)
    forward(0)
    prepare(2)
    forward(1)
    prepare(3)
    sent(0)
    forward(2)
    prepare(4)
    sent(1)
    forward(3)
    prepare(5)
    arrived(0)
    arrived(1)
    arrived(2)
    sent(2)
    forward(4)
    reduce(0)
    arrived(3)
    sent(3)
    forward(5)
    reduce(1)
    arrived(4)
    reduce(2)
    arrived(5)
    reduce(3)
    sent(4)
    sent(5)
    half_copy(na - 1).wait_send()
    for m in range(na):
        for d in range(1, NX):
            x_copy(m, d).wait_send()
        for d in range(1, NY):
            yr_copy(m, d).wait_send()
        for d in range(1, NZ):
            zr_copy(m, d).wait_send()
    for i in range(total):
        for h in range(2):
            @pl.loop(0, NZ)
            def _(zd):
                y_copy(i, h, zd).wait_send()


def body(ampl, integrals, residual_in, vir_energy, slab_energy, pair_energy):
    DMA = pltpu.SemaphoreType.DMA
    nw, na = len(W_CHUNKS), len(A_CHUNKS)
    parts = pl.pallas_call(
        kernel,
        out_shape=jax.ShapeDtypeStruct((na, 32, 128), F32),
        in_specs=[pl.BlockSpec(memory_space=pl.ANY)] * 2,
        out_specs=pl.BlockSpec(memory_space=pltpu.VMEM),
        scratch_shapes=[
            pltpu.VMEM((2, 16, 32, C), BF),
            pltpu.VMEM((8, 32, C), BF),
            pltpu.VMEM((256, 256), BF),
            pltpu.VMEM((128, 128), BF),
            pltpu.VMEM((nw, 32, 16, C), BF),
            pltpu.VMEM((na - 1, 32, 16, C), BF),
            pltpu.VMEM((32, 8, C), BF),
            pltpu.VMEM((nw, 2, ZC, 16, C), BF),
            pltpu.VMEM((na - 1, 2, ZC, 16, C), BF),
            pltpu.VMEM((2, ZC, 8, C), BF),
            pltpu.VMEM((NC, 2, NZ, 32, C), BF),
            pltpu.VMEM((na - 1, NX, 2, 4, 16, C), BF),
            pltpu.VMEM((NX, 2, 4, 8, C), BF),
            pltpu.VMEM((NX, 2, 2, 64, 256), F32),
            pltpu.VMEM((NX, 2, 2, 64, 256), F32),
            pltpu.VMEM((na, NX, 2, 2, 64, 256), F32),
            pltpu.VMEM((na, NX - 1, 2, 2, 64, 256), F32),
            pltpu.VMEM((na, 2, 2, 64, 256), F32),
            pltpu.VMEM((na, NY - 1, 64, 256), F32),
            pltpu.VMEM((na, NZ, 32, 128), F32),
            pltpu.VMEM((na, NZ - 1, 32, 128), F32),
            DMA((2,)),
            DMA((nw + na, 2, NZ)), DMA((nw + na, 2, NZ)),
            DMA((nw + na, ZC)), DMA((nw + na, ZC)),
            DMA((nw + na,)),
            DMA((na,)), DMA((na,)),
            DMA((na, NX - 1)), DMA((na, NX - 1)),
            DMA((na, NY - 1)), DMA((na, NY - 1)),
            DMA((na, NZ - 1)), DMA((na, NZ - 1)),
        ],
        compiler_params=pltpu.CompilerParams(
            collective_id=0, has_side_effects=True, vmem_limit_bytes=60 * 1024 * 1024),
        cost_estimate=pl.CostEstimate(flops=2 * 1792 * 1024 * 1792, bytes_accessed=10 * 1024 * 1024, transcendentals=0),
        name="cycle",
    )(ampl, integrals)
    pieces = [parts[m, :, :4 * n].reshape(32, 4, n) for m, (_, n) in enumerate(A_CHUNKS)]
    cycle = jnp.concatenate(pieces, axis=2).reshape(32, 224).T

    local_cols = cycle.shape[1]
    columns = lax.axis_index("col") * local_cols + jnp.arange(local_cols, dtype=jnp.int32)
    slab_index = columns % SLAB
    occ_index = columns // SLAB
    slab_local = jnp.sum(
        jnp.where(slab_index[:, None] == jnp.arange(SLAB, dtype=jnp.int32)[None, :], slab_energy[None, :], 0.0), axis=1)
    pair_local = jnp.sum(
        jnp.where(occ_index[:, None] == jnp.arange(JWIN, dtype=jnp.int32)[None, :], pair_energy[None, :], 0.0), axis=1)
    denom = vir_energy[:, None] + (slab_local - pair_local)[None, :]
    return (residual_in + cycle) / denom


def solution(mesh):
    in_specs = (P("col", "row", None), P("col", "row", None), P("row", "col"), P("row"), P(), P())
    return jax.shard_map(body, mesh=mesh, in_specs=in_specs, out_specs=P("row", "col"), check_vma=False)
```

```python
import functools

import jax
import jax.numpy as jnp
from jax import lax
from jax.experimental import pallas as pl
from jax.experimental.pallas import tpu as pltpu
from jax.sharding import PartitionSpec as P

SLAB = 128
JWIN = 8
MESH = pl.DeviceIdType.MESH
BF = jnp.bfloat16
F32 = jnp.float32
NX, NY, NZ, NC = 4, 4, 8, 2
ZC = NZ * NC
C = 1792
A_CHUNKS = ((0, 16), (16, 16), (32, 16), (48, 8))
W_CHUNKS = ((0, 16), (16, 16))


def device(x, y, z, c):
    return ((y % 2) * NX + x, ((y // 2) * NZ + z) * NC + c)


def far_first(j):
    return jnp.where(j == NZ - 1, 0, jnp.where(j % 2 == 1, 4 - (j + 1) // 2, 4 + j // 2))


def permutation(rows):
    n = rows * 16
    out = lax.broadcasted_iota(jnp.int32, (n, n), 0)
    inp = lax.broadcasted_iota(jnp.int32, (n, n), 1)
    hit = (out // rows == inp % 16) & (out % rows == inp // 16)
    return jnp.where(hit, 1.0, 0.0).astype(BF)


def kernel(ampl, integ, out0, xbuf, x3buf, perm, perm3, sw, sa, sa3, yw, ya, ya3, rw, ra, ra3,
           half, own, r1, xyr, zb, zr,
           load_sem, ys, yrv, zs, zrv, loc_sem, s0s, s0r, s1s, s1r, s3s, s3r):
    row = lax.axis_index("row")
    col = lax.axis_index("col")
    ylo, x = row // NX, row % NX
    yhi, z, c = col // ZC, (col // NC) % NZ, col % NC
    y = yhi * 2 + ylo
    zc = z * NC + c

    chunks = [(integ, s, n, sw.at[i], yw.at[i]) for i, (s, n) in enumerate(W_CHUNKS)]
    chunks += [(ampl, s, n, sa.at[i], ya.at[i]) for i, (s, n) in enumerate(A_CHUNKS[:-1])]
    chunks += [(ampl, *A_CHUNKS[-1], sa3, ya3)]
    nw, na = len(W_CHUNKS), len(A_CHUNKS)

    def load(i):
        src, start, rows, _, _ = chunks[i]
        dst = xbuf.at[i % 2] if rows == 16 else x3buf
        return pltpu.make_async_copy(src.at[pl.ds(start, rows)], dst, load_sem.at[i % 2])

    def relayout(i, h):
        _, _, rows, send, _ = chunks[i]

        @pl.loop(0, C // 256)
        def _(j):
            lanes = pl.ds(pl.multiple_of(j * 256, 256), 256)
            if rows == 16:
                block = xbuf[i % 2, :, 16 * h:16 * h + 16, lanes].reshape(256, 256)
                moved = jnp.dot(perm[...], block, preferred_element_type=F32)
                send[16 * h:16 * h + 16, :, lanes] = moved.astype(BF).reshape(16, 16, 256)
            else:
                block = x3buf[:, 16 * h:16 * h + 16, lanes].reshape(128, 256)
                moved = jnp.dot(perm3[...], block, preferred_element_type=F32)
                send[16 * h:16 * h + 16, :, lanes] = moved.reshape(16, rows, 256).astype(BF)

    def y_copy(i, h, zd):
        _, _, _, send, recv = chunks[i]
        return pltpu.make_async_remote_copy(
            src_ref=send.at[pl.ds(h * ZC + zd * NC, NC)],
            dst_ref=recv.at[yhi, pl.ds(zd * NC, NC)],
            send_sem=ys.at[i, h, zd],
            recv_sem=yrv.at[i, yhi, zd],
            device_id=device(x, h * 2 + 1 - ylo, z, c),
            device_id_type=MESH,
        )

    def y_arrived(i, h, zd):
        _, _, _, send, recv = chunks[i]
        return pltpu.make_async_copy(
            send.at[pl.ds(h * ZC + zd * NC, NC)], recv.at[h, pl.ds(zd * NC, NC)], yrv.at[i, h, zd])

    def slot(i, zz, cc):
        if i < nw:
            return rw.at[cc, :, zz, pl.ds(W_CHUNKS[i][0], 16)]
        xa, q = zz // 2, (zz % 2) * 2 + cc
        if i < nw + na - 1:
            return ra.at[i - nw, xa, :, q]
        return ra3.at[xa, :, q]

    def z_copy(i, zd, cd):
        recv = chunks[i][4]
        kk = zd * NC + cd
        return pltpu.make_async_remote_copy(
            src_ref=recv.at[:, kk],
            dst_ref=slot(i, z, c),
            send_sem=zs.at[i, kk],
            recv_sem=zrv.at[i, zc],
            device_id=device(x, y, zd, cd),
            device_id_type=MESH,
        )

    def z_arrived(i, zz, cc):
        recv = chunks[i][4]
        return pltpu.make_async_copy(recv.at[:, zz * NC + cc], slot(i, zz, cc), zrv.at[i, zz * NC + cc])

    def own_copy(i):
        return pltpu.make_async_copy(chunks[i][4].at[:, zc], slot(i, z, c), loc_sem.at[i])

    def prepare(i):
        load(i).wait()
        for h in range(2):
            relayout(i, h)
            if i == 0 and h == 0:
                meet()

            @pl.loop(0, NZ)
            def _(j):
                y_copy(i, h, (z + far_first(j)) % NZ).start()

        if i + 2 < nw + na:
            load(i + 2).start()

    def forward(i):
        @pl.loop(0, NZ - 1)
        def _(j):
            zd = (z + far_first(j)) % NZ
            for h in range(2):
                y_arrived(i, h, zd).wait()
            for cd in range(NC):
                z_copy(i, zd, cd).start()

        for h in range(2):
            y_arrived(i, h, z).wait()
        z_copy(i, z, 1 - c).start()
        own_copy(i).start()

    def sent(i):
        @pl.loop(0, NZ - 1)
        def _(j):
            zd = (z + far_first(j)) % NZ
            for cd in range(NC):
                z_copy(i, zd, cd).wait_send()

        z_copy(i, z, 1 - c).wait_send()

    def arrived(i):
        @pl.loop(0, NZ - 1)
        def _(j):
            zz = (z + far_first(j)) % NZ
            for cc in range(NC):
                z_arrived(i, zz, cc).wait()

        z_arrived(i, z, 1 - c).wait()
        own_copy(i).wait()

    def meet():
        barrier = pltpu.get_barrier_semaphore()
        for off in range(1, NX * NY):
            peer = device((x + off // NY) % NX, (y + off % NY) % NY, z, c)
            pl.semaphore_signal(barrier, inc=1, device_id=peer, device_id_type=MESH)
        for d in range(1, NZ):
            for cd in range(NC):
                pl.semaphore_signal(barrier, inc=1, device_id=device(x, y, (z + d) % NZ, cd), device_id_type=MESH)
        pl.semaphore_signal(barrier, inc=1, device_id=device(x, y, z, 1 - c), device_id_type=MESH)
        pl.semaphore_wait(barrier, NX * NY - 1 + (NZ - 1) * NC + 1)

    contract = (((1,), (1,)), ((), ()))

    def multiply(m, cn, dst):
        rows = A_CHUNKS[m][1]

        @pl.loop(0, 2)
        def _(h):
            right = rw[cn, h].reshape(256, C)
            for xa in range(NX):
                if rows == 16:
                    left = ra[m, xa].reshape(128, C)
                else:
                    left = ra3[xa].astype(F32).reshape(rows * 8, C).astype(BF)
                dst[xa, :, h, :rows * 4, :] = lax.dot_general(
                    left, right, contract, preferred_element_type=F32).reshape(2, rows * 4, 256)

    def half_copy(m):
        n = A_CHUNKS[m][1] * 4
        return pltpu.make_async_remote_copy(
            src_ref=half.at[:, :, :, pl.ds(0, n)], dst_ref=r1.at[m, :, :, :, pl.ds(0, n)],
            send_sem=s0s.at[m], recv_sem=s0r.at[m],
            device_id=device(x, y, z, 1 - c), device_id_type=MESH)

    def xy_copy(m, off):
        n = A_CHUNKS[m][1] * 4
        xd, yd = (x + off // NY) % NX, (y + off % NY) % NY
        return pltpu.make_async_remote_copy(
            src_ref=r1.at[m, xd, yd % 2, yd // 2, pl.ds(0, n)], dst_ref=xyr.at[m, off - 1, pl.ds(0, n)],
            send_sem=s1s.at[m, off - 1], recv_sem=s1r.at[m, off - 1],
            device_id=device(xd, yd, z, c), device_id_type=MESH)

    def zr_copy(g, j):
        off = far_first(j)
        zd = (z + off) % NZ
        return pltpu.make_async_remote_copy(
            src_ref=zb.at[g, zd], dst_ref=zr.at[g, off - 1],
            send_sem=s3s.at[g, off - 1], recv_sem=s3r.at[g, off - 1],
            device_id=device(x, y, zd, c), device_id_type=MESH)

    def pair_stage(m):
        n = A_CHUNKS[m][1] * 4
        if m > 0:
            half_copy(m - 1).wait_send()
        multiply(m, 1 - c, half)
        half_copy(m).start()
        multiply(m, c, own)
        half_copy(m).wait_recv()
        for d in (2, 1, 3, 0):
            xd = (x + d) % NX
            r1[m, xd, :, :, :n] = r1[m, xd, :, :, :n] + own[xd, :, :, :n]

            @pl.loop(0 if d > 0 else 1, NY)
            def _(j):
                xy_copy(m, d * NY + j).start()

    def gathered(m):
        n = A_CHUNKS[m][1] * 4

        @pl.loop(1, NX * NY)
        def _(off):
            xy_copy(m, off).wait_recv()

        total = r1[m, x, ylo, yhi, :n]
        for off in range(1, NX * NY):
            total = total + xyr[m, off - 1, :n]
        if n < 64:
            total = jnp.concatenate([total, jnp.zeros_like(total)], axis=0)
        return total

    def plane_stage(g):
        both = jnp.concatenate([gathered(2 * g), gathered(2 * g + 1)], axis=0)
        zb[g] = both.T.reshape(NZ, 32, 128)

        @pl.loop(0, NZ - 1)
        def _(j):
            zr_copy(g, j).start()

    def last_stage(g):
        @pl.loop(0, NZ - 1)
        def _(j):
            zr_copy(g, j).wait_recv()

        final = zb[g, z]
        for d in range(1, NZ):
            final = final + zr[g, d - 1]
        out0[g] = final

    load(0).start()
    load(1).start()
    perm[...] = permutation(16)
    perm3[...] = permutation(8)

    prepare(0)
    prepare(1)
    forward(0)
    prepare(2)
    forward(1)
    prepare(3)
    sent(0)
    forward(2)
    prepare(4)
    sent(1)
    forward(3)
    prepare(5)
    arrived(0)
    arrived(1)
    arrived(2)
    sent(2)
    forward(4)
    pair_stage(0)
    arrived(3)
    sent(3)
    forward(5)
    pair_stage(1)
    plane_stage(0)
    arrived(4)
    pair_stage(2)
    arrived(5)
    pair_stage(3)
    plane_stage(1)
    last_stage(0)
    last_stage(1)

    sent(4)
    sent(5)
    half_copy(na - 1).wait_send()
    for m in range(na):
        @pl.loop(1, NX * NY)
        def _(off):
            xy_copy(m, off).wait_send()
    for g in range(na // 2):
        @pl.loop(0, NZ - 1)
        def _(j):
            zr_copy(g, j).wait_send()
    for i in range(nw + na):
        for h in range(2):
            @pl.loop(0, NZ)
            def _(zd):
                y_copy(i, h, zd).wait_send()


def body(ampl, integrals, residual_in, vir_energy, slab_energy, pair_energy):
    DMA = pltpu.SemaphoreType.DMA
    nw, na = len(W_CHUNKS), len(A_CHUNKS)
    parts = pl.pallas_call(
        kernel,
        out_shape=jax.ShapeDtypeStruct((na // 2, 32, 128), F32),
        in_specs=[pl.BlockSpec(memory_space=pl.ANY)] * 2,
        out_specs=pl.BlockSpec(memory_space=pltpu.VMEM),
        scratch_shapes=[
            pltpu.VMEM((2, 16, 32, C), BF),
            pltpu.VMEM((8, 32, C), BF),
            pltpu.VMEM((256, 256), BF),
            pltpu.VMEM((128, 128), BF),
            pltpu.VMEM((nw, 32, 16, C), BF),
            pltpu.VMEM((na - 1, 32, 16, C), BF),
            pltpu.VMEM((32, 8, C), BF),
            pltpu.VMEM((nw, 2, ZC, 16, C), BF),
            pltpu.VMEM((na - 1, 2, ZC, 16, C), BF),
            pltpu.VMEM((2, ZC, 8, C), BF),
            pltpu.VMEM((NC, 2, NZ, 32, C), BF),
            pltpu.VMEM((na - 1, NX, 2, 4, 16, C), BF),
            pltpu.VMEM((NX, 2, 4, 8, C), BF),
            pltpu.VMEM((NX, 2, 2, 64, 256), F32),
            pltpu.VMEM((NX, 2, 2, 64, 256), F32),
            pltpu.VMEM((na, NX, 2, 2, 64, 256), F32),
            pltpu.VMEM((na, NX * NY - 1, 64, 256), F32),
            pltpu.VMEM((na // 2, NZ, 32, 128), F32),
            pltpu.VMEM((na // 2, NZ - 1, 32, 128), F32),
            DMA((2,)),
            DMA((nw + na, 2, NZ)), DMA((nw + na, 2, NZ)),
            DMA((nw + na, ZC)), DMA((nw + na, ZC)),
            DMA((nw + na,)),
            DMA((na,)), DMA((na,)),
            DMA((na, NX * NY - 1)), DMA((na, NX * NY - 1)),
            DMA((na // 2, NZ - 1)), DMA((na // 2, NZ - 1)),
        ],
        compiler_params=pltpu.CompilerParams(
            collective_id=0, has_side_effects=True, vmem_limit_bytes=60 * 1024 * 1024),
        cost_estimate=pl.CostEstimate(flops=2 * 1792 * 1024 * 1792, bytes_accessed=10 * 1024 * 1024, transcendentals=0),
        name="cycle",
    )(ampl, integrals)
    pieces = [
        parts[m // 2, :, m % 2 * 64:m % 2 * 64 + 4 * n].reshape(32, 4, n) for m, (_, n) in enumerate(A_CHUNKS)]
    cycle = jnp.concatenate(pieces, axis=2).reshape(32, 224).T

    local_cols = cycle.shape[1]
    columns = lax.axis_index("col") * local_cols + jnp.arange(local_cols, dtype=jnp.int32)
    slab_index = columns % SLAB
    occ_index = columns // SLAB
    slab_local = jnp.sum(
        jnp.where(slab_index[:, None] == jnp.arange(SLAB, dtype=jnp.int32)[None, :], slab_energy[None, :], 0.0), axis=1)
    pair_local = jnp.sum(
        jnp.where(occ_index[:, None] == jnp.arange(JWIN, dtype=jnp.int32)[None, :], pair_energy[None, :], 0.0), axis=1)
    denom = vir_energy[:, None] + (slab_local - pair_local)[None, :]
    return (residual_in + cycle) / denom


def solution(mesh):
    in_specs = (P("col", "row", None), P("col", "row", None), P("row", "col"), P("row"), P(), P())
    return jax.shard_map(body, mesh=mesh, in_specs=in_specs, out_specs=P("row", "col"), check_vma=False)
```

```python
import functools

import jax
import jax.numpy as jnp
from jax import lax
from jax.experimental import pallas as pl
from jax.experimental.pallas import tpu as pltpu
from jax.sharding import PartitionSpec as P

SLAB = 128
JWIN = 8
MESH = pl.DeviceIdType.MESH
BF = jnp.bfloat16
F32 = jnp.float32
NX, NY, NZ, NC = 4, 4, 8, 2
ZC = NZ * NC
C = 1792
A_CHUNKS = ((0, 16), (16, 16), (32, 16), (48, 8))
W_CHUNKS = ((0, 16), (16, 16))


def device(x, y, z, c):
    return ((y % 2) * NX + x, ((y // 2) * NZ + z) * NC + c)


def far_first(j):
    return jnp.where(j == NZ - 1, 0, jnp.where(j % 2 == 1, 4 - (j + 1) // 2, 4 + j // 2))


def need_order(t):
    return jnp.where(t % 2 == 0, 3 - t // 2, 4 + t // 2)


def permutation(rows):
    n = rows * 16
    out = lax.broadcasted_iota(jnp.int32, (n, n), 0)
    inp = lax.broadcasted_iota(jnp.int32, (n, n), 1)
    hit = (out // rows == inp % 16) & (out % rows == inp // 16)
    return jnp.where(hit, 1.0, 0.0).astype(BF)


def kernel(ampl, integ, out0, xbuf, x3buf, perm, perm3, sw, sa, sa3, yw, ya, ya3, rw, ra, ra3,
           half, own, r1, xyr, zb, zr,
           load_sem, ys, yrv, zs, zrv, ws, wrv, loc_sem, s0s, s0r, s1s, s1r, s3s, s3r):
    row = lax.axis_index("row")
    col = lax.axis_index("col")
    ylo, x = row // NX, row % NX
    yhi, z, c = col // ZC, (col // NC) % NZ, col % NC
    y = yhi * 2 + ylo
    zc = z * NC + c

    chunks = [(integ, s, n, sw.at[i], yw.at[i]) for i, (s, n) in enumerate(W_CHUNKS)]
    chunks += [(ampl, s, n, sa.at[i], ya.at[i]) for i, (s, n) in enumerate(A_CHUNKS[:-1])]
    chunks += [(ampl, *A_CHUNKS[-1], sa3, ya3)]
    nw, na = len(W_CHUNKS), len(A_CHUNKS)

    def load(i):
        src, start, rows, _, _ = chunks[i]
        dst = xbuf.at[i % 2] if rows == 16 else x3buf
        return pltpu.make_async_copy(src.at[pl.ds(start, rows)], dst, load_sem.at[i % 2])

    def relayout(i, h):
        _, _, rows, send, _ = chunks[i]

        @pl.loop(0, C // 256)
        def _(j):
            lanes = pl.ds(pl.multiple_of(j * 256, 256), 256)
            if rows == 16:
                block = xbuf[i % 2, :, 16 * h:16 * h + 16, lanes].reshape(256, 256)
                moved = jnp.dot(perm[...], block, preferred_element_type=F32)
                send[16 * h:16 * h + 16, :, lanes] = moved.astype(BF).reshape(16, 16, 256)
            else:
                block = x3buf[:, 16 * h:16 * h + 16, lanes].reshape(128, 256)
                moved = jnp.dot(perm3[...], block, preferred_element_type=F32)
                send[16 * h:16 * h + 16, :, lanes] = moved.reshape(16, rows, 256).astype(BF)

    def y_copy(i, h, zd):
        _, _, _, send, recv = chunks[i]
        return pltpu.make_async_remote_copy(
            src_ref=send.at[pl.ds(h * ZC + zd * NC, NC)],
            dst_ref=recv.at[yhi, pl.ds(zd * NC, NC)],
            send_sem=ys.at[i, h, zd],
            recv_sem=yrv.at[i, yhi, zd],
            device_id=device(x, h * 2 + 1 - ylo, z, c),
            device_id_type=MESH,
        )

    def y_arrived(i, h, zd):
        _, _, _, send, recv = chunks[i]
        return pltpu.make_async_copy(
            send.at[pl.ds(h * ZC + zd * NC, NC)], recv.at[h, pl.ds(zd * NC, NC)], yrv.at[i, h, zd])

    def source(role, j):
        return (z - j if role == 0 else z + j) % NZ

    def slot(i, role, j, zz, cc):
        if i < nw:
            return rw.at[role, cc, :, zz, pl.ds(W_CHUNKS[i][0], 16)]
        if i < nw + na - 1:
            return ra.at[i - nw, role, j, :, cc]
        return ra3.at[role, j, :, cc]

    def z_copy(i, role, j, cd):
        zd = (z + j if role == 0 else z - j) % NZ
        kk = (zd - role) % NZ * NC + cd
        return pltpu.make_async_remote_copy(
            src_ref=chunks[i][4].at[:, kk],
            dst_ref=slot(i, role, j, z, c),
            send_sem=zs.at[i, role, j, cd],
            recv_sem=zrv.at[i, role, j, c],
            device_id=device(x, y, zd, cd),
            device_id_type=MESH,
        )

    def z_arrived(i, role, j, cc):
        dst = slot(i, role, j, source(role, j), cc)
        return pltpu.make_async_copy(chunks[i][4].at[:, cc], dst, zrv.at[i, role, j, cc])

    def own_copy(i, role):
        kk = (z - role) % NZ * NC + c
        return pltpu.make_async_copy(chunks[i][4].at[:, kk], slot(i, role, 0, z, c), loc_sem.at[i, role])

    def pass_copy(i, role, j, cc):
        ref = slot(i, role, j, source(role, j), cc)
        dst = slot(i, 1 - role, j, source(role, j), cc)
        return pltpu.make_async_remote_copy(
            src_ref=ref, dst_ref=dst,
            send_sem=ws.at[i, role, j, cc], recv_sem=wrv.at[i, 1 - role, j, cc],
            device_id=device(x, y, (z + 1 - 2 * role) % NZ, c), device_id_type=MESH)

    def passed(i, role, j, cc):
        zz = (z - 1 - j if role == 1 else z + 1 + j) % NZ
        dst = slot(i, role, j, zz, cc)
        return pltpu.make_async_copy(chunks[i][4].at[:, cc], dst, wrv.at[i, role, j, cc])

    def prepare(i):
        load(i).wait()
        for h in range(2):
            relayout(i, h)
            if i == 0 and h == 0:
                meet()

            @pl.loop(0, NZ)
            def _(j):
                y_copy(i, h, (z + need_order(j)) % NZ).start()

        if i + 2 < nw + na:
            load(i + 2).start()

    def forward(i):
        @pl.loop(0, 3)
        def _(t):
            j = 3 - t
            for role in range(2):
                kz = (z + j if role == 0 else z - j - 1) % NZ
                for h in range(2):
                    y_arrived(i, h, kz).wait()
                for cd in range(NC):
                    z_copy(i, role, j, cd).start()

        for role in range(2):
            for h in range(2):
                y_arrived(i, h, (z - role) % NZ).wait()
            z_copy(i, role, 0, 1 - c).start()
            own_copy(i, role).start()

    def sent(i):
        @pl.loop(1, 4)
        def _(j):
            for role in range(2):
                for cd in range(NC):
                    z_copy(i, role, j, cd).wait_send()

        for role in range(2):
            z_copy(i, role, 0, 1 - c).wait_send()

    def arrived(i, then=None):
        for role in range(2):
            z_arrived(i, role, 0, 1 - c).wait()
            own_copy(i, role).wait()
            if then is not None:
                for cc in range(NC):
                    then(i, role, 0, cc).start()

        @pl.loop(1, 4)
        def _(j):
            for role in range(2):
                for cc in range(NC):
                    z_arrived(i, role, j, cc).wait()
                    if then is not None:
                        then(i, role, j, cc).start()

    def complete(i):
        @pl.loop(0, 4)
        def _(j):
            for role in range(2):
                for cc in range(NC):
                    passed(i, role, j, cc).wait()

    def meet():
        barrier = pltpu.get_barrier_semaphore()
        for off in range(1, NX * NY):
            peer = device((x + off // NY) % NX, (y + off % NY) % NY, z, c)
            pl.semaphore_signal(barrier, inc=1, device_id=peer, device_id_type=MESH)
        for d in range(1, NZ):
            for cd in range(NC):
                pl.semaphore_signal(barrier, inc=1, device_id=device(x, y, (z + d) % NZ, cd), device_id_type=MESH)
        pl.semaphore_signal(barrier, inc=1, device_id=device(x, y, z, 1 - c), device_id_type=MESH)
        pl.semaphore_wait(barrier, NX * NY - 1 + (NZ - 1) * NC + 1)

    contract = (((1,), (1,)), ((), ()))

    def multiply(m, cn, dst):
        rows = A_CHUNKS[m][1]
        n = rows * 2

        @pl.loop(0, 2)
        def _(h):
            parts = []
            for role in range(2):
                if rows == 16:
                    left = ra[m, role].reshape(256, C)
                else:
                    left = ra3[role].astype(F32).reshape(rows * 16, C).astype(BF)
                part = lax.dot_general(
                    left, rw[role, cn, h].reshape(256, C), contract, preferred_element_type=F32)
                parts.append(part.reshape(4, 2, n, 256))
            for role in range(2):
                for j in range(1, 4):
                    zz = source(role, j)
                    dst[zz // 2, :, h, zz % 2, :n, :] = parts[role][j]
            dst[z // 2, :, h, z % 2, :n, :] = parts[0][0] + parts[1][0]
            zz = (z + 4) % NZ
            dst[zz // 2, :, h, zz % 2, :n, :] = jnp.zeros((2, n, 256), F32)

    def half_copy(m):
        n = A_CHUNKS[m][1] * 2
        return pltpu.make_async_remote_copy(
            src_ref=half.at[:, :, :, :, pl.ds(0, n)], dst_ref=r1.at[m, :, :, :, :, pl.ds(0, n)],
            send_sem=s0s.at[m], recv_sem=s0r.at[m],
            device_id=device(x, y, z, 1 - c), device_id_type=MESH)

    def xy_copy(m, off):
        n = A_CHUNKS[m][1] * 2
        xd, yd = (x + off // NY) % NX, (y + off % NY) % NY
        return pltpu.make_async_remote_copy(
            src_ref=r1.at[m, xd, yd % 2, yd // 2, :, pl.ds(0, n)], dst_ref=xyr.at[m, off - 1, :, pl.ds(0, n)],
            send_sem=s1s.at[m, off - 1], recv_sem=s1r.at[m, off - 1],
            device_id=device(xd, yd, z, c), device_id_type=MESH)

    def zr_copy(g, j):
        off = far_first(j)
        zd = (z + off) % NZ
        return pltpu.make_async_remote_copy(
            src_ref=zb.at[g, zd], dst_ref=zr.at[g, off - 1],
            send_sem=s3s.at[g, off - 1], recv_sem=s3r.at[g, off - 1],
            device_id=device(x, y, zd, c), device_id_type=MESH)

    def pair_stage(m):
        n = A_CHUNKS[m][1] * 2
        if m > 0:
            half_copy(m - 1).wait_send()
        multiply(m, 1 - c, half)
        half_copy(m).start()
        multiply(m, c, own)
        half_copy(m).wait_recv()
        for d in (2, 1, 3, 0):
            xd = (x + d) % NX
            r1[m, xd, :, :, :, :n] = r1[m, xd, :, :, :, :n] + own[xd, :, :, :, :n]

            @pl.loop(0 if d > 0 else 1, NY)
            def _(j):
                xy_copy(m, d * NY + j).start()

    def gathered(m):
        n = A_CHUNKS[m][1] * 2

        @pl.loop(1, NX * NY)
        def _(off):
            xy_copy(m, off).wait_recv()

        total = r1[m, x, ylo, yhi, :, :n]
        for off in range(1, NX * NY):
            total = total + xyr[m, off - 1, :, :n]
        total = total.reshape(2 * n, 256)
        if n < 32:
            total = jnp.concatenate([total, jnp.zeros_like(total)], axis=0)
        return total

    def plane_stage(g):
        both = jnp.concatenate([gathered(2 * g), gathered(2 * g + 1)], axis=0)
        zb[g] = both.T.reshape(NZ, 32, 128)

        @pl.loop(0, NZ - 1)
        def _(j):
            zr_copy(g, j).start()

    def last_stage(g):
        @pl.loop(0, NZ - 1)
        def _(j):
            zr_copy(g, j).wait_recv()

        final = zb[g, z]
        for d in range(1, NZ):
            final = final + zr[g, d - 1]
        out0[g] = final

    load(0).start()
    load(1).start()
    perm[...] = permutation(16)
    perm3[...] = permutation(8)

    prepare(0)
    prepare(1)
    forward(0)
    prepare(2)
    forward(1)
    prepare(3)
    arrived(0, pass_copy)
    sent(0)
    forward(2)
    prepare(4)
    arrived(1, pass_copy)
    sent(1)
    forward(3)
    prepare(5)
    complete(0)
    complete(1)
    arrived(2)
    sent(2)
    forward(4)
    pair_stage(0)
    arrived(3)
    sent(3)
    forward(5)
    pair_stage(1)
    plane_stage(0)
    arrived(4)
    pair_stage(2)
    arrived(5)
    pair_stage(3)
    plane_stage(1)
    last_stage(0)
    last_stage(1)

    sent(4)
    sent(5)
    half_copy(na - 1).wait_send()
    for m in range(na):
        @pl.loop(1, NX * NY)
        def _(off):
            xy_copy(m, off).wait_send()
    for g in range(na // 2):
        @pl.loop(0, NZ - 1)
        def _(j):
            zr_copy(g, j).wait_send()
    for i in range(nw):
        @pl.loop(0, 4)
        def _(j):
            for role in range(2):
                for cc in range(NC):
                    pass_copy(i, role, j, cc).wait_send()
    for i in range(nw + na):
        for h in range(2):
            @pl.loop(0, NZ)
            def _(zd):
                y_copy(i, h, zd).wait_send()


def body(ampl, integrals, residual_in, vir_energy, slab_energy, pair_energy):
    DMA = pltpu.SemaphoreType.DMA
    nw, na = len(W_CHUNKS), len(A_CHUNKS)
    parts = pl.pallas_call(
        kernel,
        out_shape=jax.ShapeDtypeStruct((na // 2, 32, 128), F32),
        in_specs=[pl.BlockSpec(memory_space=pl.ANY)] * 2,
        out_specs=pl.BlockSpec(memory_space=pltpu.VMEM),
        scratch_shapes=[
            pltpu.VMEM((2, 16, 32, C), BF),
            pltpu.VMEM((8, 32, C), BF),
            pltpu.VMEM((256, 256), BF),
            pltpu.VMEM((128, 128), BF),
            pltpu.VMEM((nw, 32, 16, C), BF),
            pltpu.VMEM((na - 1, 32, 16, C), BF),
            pltpu.VMEM((32, 8, C), BF),
            pltpu.VMEM((nw, 2, ZC, 16, C), BF),
            pltpu.VMEM((na - 1, 2, ZC, 16, C), BF),
            pltpu.VMEM((2, ZC, 8, C), BF),
            pltpu.VMEM((2, NC, 2, NZ, 32, C), BF),
            pltpu.VMEM((na - 1, 2, 4, 2, NC, 16, C), BF),
            pltpu.VMEM((2, 4, 2, NC, 8, C), BF),
            pltpu.VMEM((NX, 2, 2, 2, 32, 256), F32),
            pltpu.VMEM((NX, 2, 2, 2, 32, 256), F32),
            pltpu.VMEM((na, NX, 2, 2, 2, 32, 256), F32),
            pltpu.VMEM((na, NX * NY - 1, 2, 32, 256), F32),
            pltpu.VMEM((na // 2, NZ, 32, 128), F32),
            pltpu.VMEM((na // 2, NZ - 1, 32, 128), F32),
            DMA((2,)),
            DMA((nw + na, 2, NZ)), DMA((nw + na, 2, NZ)),
            DMA((nw + na, 2, 4, NC)), DMA((nw + na, 2, 4, NC)),
            DMA((nw, 2, 4, NC)), DMA((nw, 2, 4, NC)),
            DMA((nw + na, 2)),
            DMA((na,)), DMA((na,)),
            DMA((na, NX * NY - 1)), DMA((na, NX * NY - 1)),
            DMA((na // 2, NZ - 1)), DMA((na // 2, NZ - 1)),
        ],
        compiler_params=pltpu.CompilerParams(
            collective_id=0, has_side_effects=True, vmem_limit_bytes=60 * 1024 * 1024),
        cost_estimate=pl.CostEstimate(flops=2 * 1792 * 1024 * 1792, bytes_accessed=10 * 1024 * 1024, transcendentals=0),
        name="cycle",
    )(ampl, integrals)
    pieces = [
        parts[m // 2, :, m % 2 * 64:m % 2 * 64 + 4 * n].reshape(32, 4, n) for m, (_, n) in enumerate(A_CHUNKS)]
    cycle = jnp.concatenate(pieces, axis=2).reshape(32, 224).T

    local_cols = cycle.shape[1]
    columns = lax.axis_index("col") * local_cols + jnp.arange(local_cols, dtype=jnp.int32)
    slab_index = columns % SLAB
    occ_index = columns // SLAB
    slab_local = jnp.sum(
        jnp.where(slab_index[:, None] == jnp.arange(SLAB, dtype=jnp.int32)[None, :], slab_energy[None, :], 0.0), axis=1)
    pair_local = jnp.sum(
        jnp.where(occ_index[:, None] == jnp.arange(JWIN, dtype=jnp.int32)[None, :], pair_energy[None, :], 0.0), axis=1)
    denom = vir_energy[:, None] + (slab_local - pair_local)[None, :]
    return (residual_in + cycle) / denom


def solution(mesh):
    in_specs = (P("col", "row", None), P("col", "row", None), P("row", "col"), P("row"), P(), P())
    return jax.shard_map(body, mesh=mesh, in_specs=in_specs, out_specs=P("row", "col"), check_vma=False)
```

```python
import functools

import jax
import jax.numpy as jnp
from jax import lax
from jax.experimental import pallas as pl
from jax.experimental.pallas import tpu as pltpu
from jax.sharding import PartitionSpec as P

SLAB = 128
JWIN = 8
MESH = pl.DeviceIdType.MESH
BF = jnp.bfloat16
F32 = jnp.float32
NX, NY, NZ, NC = 4, 4, 8, 2
ZC = NZ * NC
C = 1792
A_CHUNKS = ((0, 16), (16, 16), (32, 16), (48, 8))
W_CHUNKS = ((0, 16), (16, 16))


def device(x, y, z, c):
    return ((y % 2) * NX + x, ((y // 2) * NZ + z) * NC + c)


def far_first(j):
    return jnp.where(j == NZ - 1, 0, jnp.where(j % 2 == 1, 4 - (j + 1) // 2, 4 + j // 2))


def need_order(t):
    return jnp.where(t % 2 == 0, 3 - t // 2, 4 + t // 2)


def permutation(rows):
    n = rows * 16
    bits = rows.bit_length() - 1
    out = lax.broadcasted_iota(jnp.int32, (n, n), 0)
    inp = lax.broadcasted_iota(jnp.int32, (n, n), 1)
    hit = ((out >> bits) == (inp & 15)) & ((out & (rows - 1)) == (inp >> 4))
    return jnp.where(hit, 1.0, 0.0).astype(BF)


def kernel(ampl, integ, residual, vir, slab, pair, out, xbuf, x3buf, perm, perm3, sw, sa, sa3, yw, ya, ya3, rw, ra, ra3,
           half, own, r1, xyr, zb, zr, res_v, vir_v, slab_v, pair_v,
           load_sem, first_sem, small_sem, ys, yrv, zs, zrv, ws, wrv, loc_sem, s0s, s0r, s1s, s1r, s3s, s3r):
    row = lax.axis_index("row")
    col = lax.axis_index("col")
    ylo, x = row // NX, row % NX
    yhi, z, c = col // ZC, (col // NC) % NZ, col % NC
    y = yhi * 2 + ylo
    zc = z * NC + c

    chunks = [(integ, s, n, sw.at[i], yw.at[i]) for i, (s, n) in enumerate(W_CHUNKS)]
    chunks += [(ampl, s, n, sa.at[i], ya.at[i]) for i, (s, n) in enumerate(A_CHUNKS[:-1])]
    chunks += [(ampl, *A_CHUNKS[-1], sa3, ya3)]
    nw, na = len(W_CHUNKS), len(A_CHUNKS)

    def load(i):
        src, start, rows, _, _ = chunks[i]
        dst = xbuf.at[i % 2] if rows == 16 else x3buf
        return pltpu.make_async_copy(src.at[pl.ds(start, rows)], dst, load_sem.at[i % 2])

    def first_load(h):
        ks = pl.ds(16 * h, 16)
        return pltpu.make_async_copy(integ.at[pl.ds(0, 16), ks], xbuf.at[0, :, ks], first_sem.at[h])

    def relayout(i, h):
        _, _, rows, send, _ = chunks[i]

        @pl.loop(0, C // 256)
        def _(j):
            lanes = pl.ds(pl.multiple_of(j * 256, 256), 256)
            if rows == 16:
                block = xbuf[i % 2, :, 16 * h:16 * h + 16, lanes].reshape(256, 256)
                moved = jnp.dot(perm[...], block, preferred_element_type=F32)
                send[16 * h:16 * h + 16, :, lanes] = moved.astype(BF).reshape(16, 16, 256)
            else:
                block = x3buf[:, 16 * h:16 * h + 16, lanes].reshape(128, 256)
                moved = jnp.dot(perm3[...], block, preferred_element_type=F32)
                send[16 * h:16 * h + 16, :, lanes] = moved.reshape(16, rows, 256).astype(BF)

    def y_copy(i, h, zd):
        _, _, _, send, recv = chunks[i]
        return pltpu.make_async_remote_copy(
            src_ref=send.at[pl.ds(h * ZC + zd * NC, NC)],
            dst_ref=recv.at[yhi, pl.ds(zd * NC, NC)],
            send_sem=ys.at[i, h, zd],
            recv_sem=yrv.at[i, yhi, zd],
            device_id=device(x, h * 2 + 1 - ylo, z, c),
            device_id_type=MESH,
        )

    def y_arrived(i, h, zd):
        _, _, _, send, recv = chunks[i]
        return pltpu.make_async_copy(
            send.at[pl.ds(h * ZC + zd * NC, NC)], recv.at[h, pl.ds(zd * NC, NC)], yrv.at[i, h, zd])

    def source(role, j):
        return (z - j if role == 0 else z + j) % NZ

    def slot(i, role, j, zz, cc):
        if i < nw:
            return rw.at[role, cc, :, zz, pl.ds(W_CHUNKS[i][0], 16)]
        if i < nw + na - 1:
            return ra.at[i - nw, role, j, :, cc]
        return ra3.at[role, j, :, cc]

    def z_copy(i, role, j, cd):
        zd = (z + j if role == 0 else z - j) % NZ
        kk = (zd - role) % NZ * NC + cd
        return pltpu.make_async_remote_copy(
            src_ref=chunks[i][4].at[:, kk],
            dst_ref=slot(i, role, j, z, c),
            send_sem=zs.at[i, role, j, cd],
            recv_sem=zrv.at[i, role, j, c],
            device_id=device(x, y, zd, cd),
            device_id_type=MESH,
        )

    def z_arrived(i, role, j, cc):
        dst = slot(i, role, j, source(role, j), cc)
        return pltpu.make_async_copy(chunks[i][4].at[:, cc], dst, zrv.at[i, role, j, cc])

    def own_copy(i, role):
        kk = (z - role) % NZ * NC + c
        return pltpu.make_async_copy(chunks[i][4].at[:, kk], slot(i, role, 0, z, c), loc_sem.at[i, role])

    def pass_copy(i, role, j, cc):
        ref = slot(i, role, j, source(role, j), cc)
        dst = slot(i, 1 - role, j, source(role, j), cc)
        return pltpu.make_async_remote_copy(
            src_ref=ref, dst_ref=dst,
            send_sem=ws.at[i, role, j, cc], recv_sem=wrv.at[i, 1 - role, j, cc],
            device_id=device(x, y, (z + 1 - 2 * role) % NZ, c), device_id_type=MESH)

    def passed(i, role, j, cc):
        zz = (z - 1 - j if role == 1 else z + 1 + j) % NZ
        dst = slot(i, role, j, zz, cc)
        return pltpu.make_async_copy(chunks[i][4].at[:, cc], dst, wrv.at[i, role, j, cc])

    def prepare(i):
        if i > 0:
            load(i).wait()
        for h in range(2):
            if i == 0:
                first_load(h).wait()
            relayout(i, h)
            if i == 0 and h == 0:
                pl.semaphore_wait(barrier, NX * NY - 1 + (NZ - 1) * NC + 1)

            @pl.loop(0, NZ)
            def _(j):
                y_copy(i, h, (z + need_order(j)) % NZ).start()

        if i + 2 < nw + na:
            load(i + 2).start()

    def forward(i):
        @pl.loop(0, 3)
        def _(t):
            j = 3 - t
            for role in range(2):
                kz = (z + j if role == 0 else z - j - 1) % NZ
                for h in range(2):
                    y_arrived(i, h, kz).wait()
                for cd in range(NC):
                    z_copy(i, role, j, cd).start()

        for role in range(2):
            for h in range(2):
                y_arrived(i, h, (z - role) % NZ).wait()
            z_copy(i, role, 0, 1 - c).start()
            own_copy(i, role).start()

    def sent(i):
        @pl.loop(1, 4)
        def _(j):
            for role in range(2):
                for cd in range(NC):
                    z_copy(i, role, j, cd).wait_send()

        for role in range(2):
            z_copy(i, role, 0, 1 - c).wait_send()

    def arrived(i, then=None):
        for role in range(2):
            z_arrived(i, role, 0, 1 - c).wait()
            own_copy(i, role).wait()
            if then is not None:
                for cc in range(NC):
                    then(i, role, 0, cc).start()

        @pl.loop(1, 4)
        def _(j):
            for role in range(2):
                for cc in range(NC):
                    z_arrived(i, role, j, cc).wait()
                    if then is not None:
                        then(i, role, j, cc).start()

    def complete(i):
        @pl.loop(0, 4)
        def _(j):
            for role in range(2):
                for cc in range(NC):
                    passed(i, role, j, cc).wait()

    contract = (((1,), (1,)), ((), ()))

    def multiply(m, cn, dst, h):
        rows = A_CHUNKS[m][1]
        n = rows * 2

        parts = []
        for role in range(2):
            if rows == 16:
                left = ra[m, role].reshape(256, C)
            else:
                left = ra3[role].astype(F32).reshape(rows * 16, C).astype(BF)
            part = lax.dot_general(
                left, rw[role, cn, h].reshape(256, C), contract, preferred_element_type=F32)
            parts.append(part.reshape(4, 2, n, 256))
        for role in range(2):
            for j in range(1, 4):
                zz = source(role, j)
                dst[zz // 2, :, h, zz % 2, :n, :] = parts[role][j]
        dst[z // 2, :, h, z % 2, :n, :] = parts[0][0] + parts[1][0]
        zz = (z + 4) % NZ
        dst[zz // 2, :, h, zz % 2, :n, :] = jnp.zeros((2, n, 256), F32)

    def half_copy(m, h):
        n = A_CHUNKS[m][1] * 2
        return pltpu.make_async_remote_copy(
            src_ref=half.at[:, :, h, :, pl.ds(0, n)], dst_ref=r1.at[m, :, :, h, :, pl.ds(0, n)],
            send_sem=s0s.at[m, h], recv_sem=s0r.at[m, h],
            device_id=device(x, y, z, 1 - c), device_id_type=MESH)

    def xy_copy(m, off):
        n = A_CHUNKS[m][1] * 2
        xd, yd = (x + off // NY) % NX, (y + off % NY) % NY
        return pltpu.make_async_remote_copy(
            src_ref=r1.at[m, xd, yd % 2, yd // 2, :, pl.ds(0, n)], dst_ref=xyr.at[m, off - 1, :, pl.ds(0, n)],
            send_sem=s1s.at[m, off - 1], recv_sem=s1r.at[m, off - 1],
            device_id=device(xd, yd, z, c), device_id_type=MESH)

    def zr_copy(m, j):
        n = A_CHUNKS[m][1]
        off = far_first(j)
        zd = (z + off) % NZ
        return pltpu.make_async_remote_copy(
            src_ref=zb.at[m, zd, pl.ds(0, n)], dst_ref=zr.at[m, off - 1, pl.ds(0, n)],
            send_sem=s3s.at[m, off - 1], recv_sem=s3r.at[m, off - 1],
            device_id=device(x, y, zd, c), device_id_type=MESH)

    def pair_stage(m):
        n = A_CHUNKS[m][1] * 2
        if m > 0:
            for h in range(2):
                half_copy(m - 1, h).wait_send()

        @pl.loop(0, 2)
        def _(h):
            multiply(m, 1 - c, half, h)
            half_copy(m, h).start()

        @pl.loop(0, 2)
        def _(h):
            multiply(m, c, own, h)

        @pl.loop(0, 2)
        def _(h):
            half_copy(m, h).wait_recv()
            for d in (2, 1, 3, 0):
                xd = (x + d) % NX
                r1[m, xd, :, h, :, :n] = r1[m, xd, :, h, :, :n] + own[xd, :, h, :, :n]
                for b in range(2):
                    dy = (h * 2 + b - y + NY) % NY
                    if d > 0:
                        xy_copy(m, d * NY + dy).start()
                    else:
                        @pl.when(dy > 0)
                        def _():
                            xy_copy(m, dy).start()

    def plane_stage(m):
        n = A_CHUNKS[m][1]

        @pl.loop(1, NX * NY)
        def _(off):
            xy_copy(m, off).wait_recv()

        total = r1[m, x, ylo, yhi, :, :2 * n]
        for off in range(1, NX * NY):
            total = total + xyr[m, off - 1, :, :2 * n]
        total = total.reshape(4 * n, 256)
        for zd in range(NZ):
            zb[m, zd, :n] = jnp.concatenate(
                [total[n * q:n * q + n, 32 * zd:32 * zd + 32] for q in range(4)], axis=1)

        @pl.loop(0, NZ - 1)
        def _(j):
            zr_copy(m, j).start()

    def last_stage(m):
        n = A_CHUNKS[m][1]

        @pl.loop(0, NZ - 1)
        def _(j):
            zr_copy(m, j).wait_recv()

        final = zb[m, z, :n]
        for d in range(1, NZ):
            final = final + zr[m, d - 1, :n]
        return final

    def finish():
        for cp in small_loads:
            cp.wait()
        finals = [last_stage(m) for m in range(na)]
        cycle = jnp.concatenate(
            [finals[m][:, 32 * q:32 * q + 32] for q in range(4) for m in range(na)], axis=0).T
        lane = lax.broadcasted_iota(jnp.int32, (32, SLAB), 1)
        line = lax.broadcasted_iota(jnp.int32, (32, SLAB), 0)
        wanted = lane == (col % 4) * 32 + line
        slab_col = jnp.sum(jnp.where(wanted, slab_v[...], 0.0), axis=1, keepdims=True)
        which = lax.broadcasted_iota(jnp.int32, (1, JWIN), 1) == col // 4
        pair_col = jnp.sum(jnp.where(which, pair_v[...], 0.0), axis=1, keepdims=True)
        denom = vir_v[...] + (slab_col - pair_col)
        out[...] = (res_v[...] + cycle) / denom

    for h in range(2):
        first_load(h).start()
    barrier = pltpu.get_barrier_semaphore()
    for off in range(1, NX * NY):
        peer = device((x + off // NY) % NX, (y + off % NY) % NY, z, c)
        pl.semaphore_signal(barrier, inc=1, device_id=peer, device_id_type=MESH)
    for d in range(1, NZ):
        for cd in range(NC):
            pl.semaphore_signal(barrier, inc=1, device_id=device(x, y, (z + d) % NZ, cd), device_id_type=MESH)
    pl.semaphore_signal(barrier, inc=1, device_id=device(x, y, z, 1 - c), device_id_type=MESH)
    load(1).start()
    small_loads = [
        pltpu.make_async_copy(src, dst, small_sem.at[i])
        for i, (src, dst) in enumerate(((residual, res_v), (vir, vir_v), (slab, slab_v), (pair, pair_v)))]
    for cp in small_loads:
        cp.start()
    perm[...] = permutation(16)
    perm3[...] = permutation(8)

    prepare(0)
    prepare(1)
    forward(0)
    prepare(2)
    forward(1)
    prepare(3)
    arrived(0, pass_copy)
    sent(0)
    forward(2)
    prepare(4)
    arrived(1, pass_copy)
    sent(1)
    forward(3)
    prepare(5)
    complete(0)
    complete(1)
    arrived(2)
    sent(2)
    forward(4)
    pair_stage(0)
    arrived(3)
    sent(3)
    forward(5)
    pair_stage(1)
    plane_stage(0)
    arrived(4)
    pair_stage(2)
    plane_stage(1)
    arrived(5)
    pair_stage(3)
    plane_stage(2)
    plane_stage(3)
    finish()
    sent(4)
    sent(5)
    for h in range(2):
        half_copy(na - 1, h).wait_send()
    for m in range(na):
        @pl.loop(1, NX * NY)
        def _(off):
            xy_copy(m, off).wait_send()
    for m in range(na):
        @pl.loop(0, NZ - 1)
        def _(j):
            zr_copy(m, j).wait_send()
    for i in range(nw):
        @pl.loop(0, 4)
        def _(j):
            for role in range(2):
                for cc in range(NC):
                    pass_copy(i, role, j, cc).wait_send()
    for i in range(nw + na):
        for h in range(2):
            @pl.loop(0, NZ)
            def _(zd):
                y_copy(i, h, zd).wait_send()


def body(ampl, integrals, residual_in, vir_energy, slab_energy, pair_energy):
    DMA = pltpu.SemaphoreType.DMA
    nw, na = len(W_CHUNKS), len(A_CHUNKS)
    update = pl.pallas_call(
        kernel,
        out_shape=jax.ShapeDtypeStruct((32, 224), F32),
        in_specs=[pl.BlockSpec(memory_space=pl.ANY)] * 6,
        out_specs=pl.BlockSpec(memory_space=pltpu.VMEM),
        scratch_shapes=[
            pltpu.VMEM((2, 16, 32, C), BF),
            pltpu.VMEM((8, 32, C), BF),
            pltpu.VMEM((256, 256), BF),
            pltpu.VMEM((128, 128), BF),
            pltpu.VMEM((nw, 32, 16, C), BF),
            pltpu.VMEM((na - 1, 32, 16, C), BF),
            pltpu.VMEM((32, 8, C), BF),
            pltpu.VMEM((nw, 2, ZC, 16, C), BF),
            pltpu.VMEM((na - 1, 2, ZC, 16, C), BF),
            pltpu.VMEM((2, ZC, 8, C), BF),
            pltpu.VMEM((2, NC, 2, NZ, 32, C), BF),
            pltpu.VMEM((na - 1, 2, 4, 2, NC, 16, C), BF),
            pltpu.VMEM((2, 4, 2, NC, 8, C), BF),
            pltpu.VMEM((NX, 2, 2, 2, 32, 256), F32),
            pltpu.VMEM((NX, 2, 2, 2, 32, 256), F32),
            pltpu.VMEM((na, NX, 2, 2, 2, 32, 256), F32),
            pltpu.VMEM((na, NX * NY - 1, 2, 32, 256), F32),
            pltpu.VMEM((na, NZ, 16, 128), F32),
            pltpu.VMEM((na, NZ - 1, 16, 128), F32),
            pltpu.VMEM((32, 224), F32),
            pltpu.VMEM((1, 224), F32),
            pltpu.VMEM((1, SLAB), F32),
            pltpu.VMEM((1, JWIN), F32),
            DMA((2,)), DMA((2,)), DMA((4,)),
            DMA((nw + na, 2, NZ)), DMA((nw + na, 2, NZ)),
            DMA((nw + na, 2, 4, NC)), DMA((nw + na, 2, 4, NC)),
            DMA((nw, 2, 4, NC)), DMA((nw, 2, 4, NC)),
            DMA((nw + na, 2)),
            DMA((na, 2)), DMA((na, 2)),
            DMA((na, NX * NY - 1)), DMA((na, NX * NY - 1)),
            DMA((na, NZ - 1)), DMA((na, NZ - 1)),
        ],
        compiler_params=pltpu.CompilerParams(
            collective_id=0, has_side_effects=True, vmem_limit_bytes=60 * 1024 * 1024),
        cost_estimate=pl.CostEstimate(flops=2 * 1792 * 1024 * 1792, bytes_accessed=10 * 1024 * 1024, transcendentals=0),
        name="cycle",
    )(ampl, integrals, residual_in.T, vir_energy[None, :], slab_energy[None, :], pair_energy[None, :])
    return update.T


def solution(mesh):
    in_specs = (P("col", "row", None), P("col", "row", None), P("row", "col"), P("row"), P(), P())
    return jax.shard_map(body, mesh=mesh, in_specs=in_specs, out_specs=P("row", "col"), check_vma=False)
```

```python
import functools

import jax
import jax.numpy as jnp
from jax import lax
from jax.experimental import pallas as pl
from jax.experimental.pallas import tpu as pltpu
from jax.sharding import PartitionSpec as P

SLAB = 128
JWIN = 8
MESH = pl.DeviceIdType.MESH
BF = jnp.bfloat16
F32 = jnp.float32
NX, NY, NZ, NC = 4, 4, 8, 2
ZC = NZ * NC
C = 1792
A_CHUNKS = ((0, 16), (16, 16), (32, 16), (48, 8))
W_CHUNKS = ((0, 16), (16, 16))


def device(x, y, z, c):
    return ((y % 2) * NX + x, ((y // 2) * NZ + z) * NC + c)


def far_first(j):
    return jnp.where(j == NZ - 1, 0, jnp.where(j % 2 == 1, 4 - (j + 1) // 2, 4 + j // 2))


def need_order(t):
    return jnp.where(t % 2 == 0, 3 - t // 2, 4 + t // 2)


def permutation(rows):
    n = rows * 16
    bits = rows.bit_length() - 1
    out = lax.broadcasted_iota(jnp.int32, (n, n), 0)
    inp = lax.broadcasted_iota(jnp.int32, (n, n), 1)
    hit = ((out >> bits) == (inp & 15)) & ((out & (rows - 1)) == (inp >> 4))
    return jnp.where(hit, 1.0, 0.0).astype(BF)


def kernel(ampl, integ, residual, vir, slab, pair, out, xbuf, x3buf, perm, perm3, sw, sa, sa3, yw, ya, ya3, rw, ra, ra3,
           half, own, r1, xyr, zb, zr, res_v, vir_v, slab_v, pair_v,
           load_sem, first_sem, small_sem, ys, yrv, zs, zrv, ws, wrv, loc_sem, s0s, s0r, s1s, s1r, s3s, s3r):
    row = lax.axis_index("row")
    col = lax.axis_index("col")
    ylo, x = row // NX, row % NX
    yhi, z, c = col // ZC, (col // NC) % NZ, col % NC
    y = yhi * 2 + ylo
    zc = z * NC + c

    chunks = [(integ, s, n, sw.at[i], yw.at[i]) for i, (s, n) in enumerate(W_CHUNKS)]
    chunks += [(ampl, s, n, sa.at[i], ya.at[i]) for i, (s, n) in enumerate(A_CHUNKS[:-1])]
    chunks += [(ampl, *A_CHUNKS[-1], sa3, ya3)]
    nw, na = len(W_CHUNKS), len(A_CHUNKS)

    def load(i):
        src, start, rows, _, _ = chunks[i]
        dst = xbuf.at[i % 2] if rows == 16 else x3buf
        return pltpu.make_async_copy(src.at[pl.ds(start, rows)], dst, load_sem.at[i % 2])

    def first_load(h):
        ks = pl.ds(16 * h, 16)
        return pltpu.make_async_copy(integ.at[pl.ds(0, 16), ks], xbuf.at[0, :, ks], first_sem.at[h])

    def relayout(i, h):
        _, _, rows, send, _ = chunks[i]

        @pl.loop(0, C // 256)
        def _(j):
            lanes = pl.ds(pl.multiple_of(j * 256, 256), 256)
            if rows == 16:
                block = xbuf[i % 2, :, 16 * h:16 * h + 16, lanes].reshape(256, 256)
                moved = jnp.dot(perm[...], block, preferred_element_type=F32)
                send[16 * h:16 * h + 16, :, lanes] = moved.astype(BF).reshape(16, 16, 256)
            else:
                block = x3buf[:, 16 * h:16 * h + 16, lanes].reshape(128, 256)
                moved = jnp.dot(perm3[...], block, preferred_element_type=F32)
                send[16 * h:16 * h + 16, :, lanes] = moved.reshape(16, rows, 256).astype(BF)

    def y_copy(i, h, zd):
        _, _, _, send, recv = chunks[i]
        return pltpu.make_async_remote_copy(
            src_ref=send.at[pl.ds(h * ZC + zd * NC, NC)],
            dst_ref=recv.at[yhi, pl.ds(zd * NC, NC)],
            send_sem=ys.at[i, h, zd],
            recv_sem=yrv.at[i, yhi, zd],
            device_id=device(x, h * 2 + 1 - ylo, z, c),
            device_id_type=MESH,
        )

    def y_arrived(i, h, zd):
        _, _, _, send, recv = chunks[i]
        return pltpu.make_async_copy(
            send.at[pl.ds(h * ZC + zd * NC, NC)], recv.at[h, pl.ds(zd * NC, NC)], yrv.at[i, h, zd])

    def source(role, j):
        return (z - j if role == 0 else z + j) % NZ

    def slot(i, role, j, zz, cc):
        if i < nw:
            return rw.at[role, cc, :, zz, pl.ds(W_CHUNKS[i][0], 16)]
        if i < nw + na - 1:
            return ra.at[i - nw, role, j, :, cc]
        return ra3.at[role, j, :, cc]

    def z_copy(i, role, j, cd):
        zd = (z + j if role == 0 else z - j) % NZ
        kk = (zd - role) % NZ * NC + cd
        return pltpu.make_async_remote_copy(
            src_ref=chunks[i][4].at[:, kk],
            dst_ref=slot(i, role, j, z, c),
            send_sem=zs.at[i, role, j, cd],
            recv_sem=zrv.at[i, role, j, c],
            device_id=device(x, y, zd, cd),
            device_id_type=MESH,
        )

    def z_arrived(i, role, j, cc):
        dst = slot(i, role, j, source(role, j), cc)
        return pltpu.make_async_copy(chunks[i][4].at[:, cc], dst, zrv.at[i, role, j, cc])

    def own_copy(i, role):
        kk = (z - role) % NZ * NC + c
        return pltpu.make_async_copy(chunks[i][4].at[:, kk], slot(i, role, 0, z, c), loc_sem.at[i, role])

    def pass_copy(i, role, j, cc):
        ref = slot(i, role, j, source(role, j), cc)
        dst = slot(i, 1 - role, j, source(role, j), cc)
        return pltpu.make_async_remote_copy(
            src_ref=ref, dst_ref=dst,
            send_sem=ws.at[i, role, j, cc], recv_sem=wrv.at[i, 1 - role, j, cc],
            device_id=device(x, y, (z + 1 - 2 * role) % NZ, c), device_id_type=MESH)

    def passed(i, role, j, cc):
        zz = (z - 1 - j if role == 1 else z + 1 + j) % NZ
        dst = slot(i, role, j, zz, cc)
        return pltpu.make_async_copy(chunks[i][4].at[:, cc], dst, wrv.at[i, role, j, cc])

    def prepare(i):
        if i > 0:
            load(i).wait()
        for h in range(2):
            if i == 0:
                first_load(h).wait()
            relayout(i, h)
            if i == 0 and h == 0:
                pl.semaphore_wait(barrier, NX * NY - 1 + (NZ - 1) * NC + 1)

            @pl.loop(0, NZ)
            def _(j):
                y_copy(i, h, (z + need_order(j)) % NZ).start()

        if i + 2 < nw + na:
            load(i + 2).start()

    def forward(i):
        @pl.loop(0, 3)
        def _(t):
            j = 3 - t
            for role in range(2):
                kz = (z + j if role == 0 else z - j - 1) % NZ
                for h in range(2):
                    y_arrived(i, h, kz).wait()
                for cd in range(NC):
                    z_copy(i, role, j, cd).start()

        for role in range(2):
            for h in range(2):
                y_arrived(i, h, (z - role) % NZ).wait()
            z_copy(i, role, 0, 1 - c).start()
            own_copy(i, role).start()

    def sent(i):
        @pl.loop(1, 4)
        def _(j):
            for role in range(2):
                for cd in range(NC):
                    z_copy(i, role, j, cd).wait_send()

        for role in range(2):
            z_copy(i, role, 0, 1 - c).wait_send()

    def arrived(i, then=None):
        for role in range(2):
            z_arrived(i, role, 0, 1 - c).wait()
            own_copy(i, role).wait()
            if then is not None:
                for cc in range(NC):
                    then(i, role, 0, cc).start()

        @pl.loop(1, 4)
        def _(j):
            for role in range(2):
                for cc in range(NC):
                    z_arrived(i, role, j, cc).wait()
                    if then is not None:
                        then(i, role, j, cc).start()

    def complete(i):
        @pl.loop(0, 4)
        def _(j):
            for role in range(2):
                for cc in range(NC):
                    passed(i, role, j, cc).wait()

    contract = (((1,), (1,)), ((), ()))

    def multiply(m, cn, dst, h):
        rows = A_CHUNKS[m][1]
        n = rows * 2

        parts = []
        for role in range(2):
            if rows == 16:
                left = ra[m, role].reshape(256, C)
            else:
                left = ra3[role].astype(F32).reshape(rows * 16, C).astype(BF)
            part = lax.dot_general(
                left, rw[role, cn, h].reshape(256, C), contract, preferred_element_type=F32)
            parts.append(part.reshape(4, 2, n, 256))
        for role in range(2):
            for j in range(1, 4):
                zz = source(role, j)
                dst[zz // 2, :, h, zz % 2, :n, :] = parts[role][j]
        dst[z // 2, :, h, z % 2, :n, :] = parts[0][0] + parts[1][0]
        zz = (z + 4) % NZ
        dst[zz // 2, :, h, zz % 2, :n, :] = jnp.zeros((2, n, 256), F32)

    def half_copy(m, h):
        n = A_CHUNKS[m][1] * 2
        return pltpu.make_async_remote_copy(
            src_ref=half.at[:, :, h, :, pl.ds(0, n)], dst_ref=r1.at[m, :, :, h, :, pl.ds(0, n)],
            send_sem=s0s.at[m, h], recv_sem=s0r.at[m, h],
            device_id=device(x, y, z, 1 - c), device_id_type=MESH)

    def xy_copy(m, off):
        n = A_CHUNKS[m][1] * 2
        xd, yd = (x + off // NY) % NX, (y + off % NY) % NY
        return pltpu.make_async_remote_copy(
            src_ref=r1.at[m, xd, yd % 2, yd // 2, :, pl.ds(0, n)], dst_ref=xyr.at[m, off - 1, :, pl.ds(0, n)],
            send_sem=s1s.at[m, off - 1], recv_sem=s1r.at[m, off - 1],
            device_id=device(xd, yd, z, c), device_id_type=MESH)

    def zr_copy(m, j):
        n = A_CHUNKS[m][1]
        off = far_first(j)
        zd = (z + off) % NZ
        return pltpu.make_async_remote_copy(
            src_ref=zb.at[m, zd, pl.ds(0, n)], dst_ref=zr.at[m, off - 1, pl.ds(0, n)],
            send_sem=s3s.at[m, off - 1], recv_sem=s3r.at[m, off - 1],
            device_id=device(x, y, zd, c), device_id_type=MESH)

    def pair_stage(m):
        n = A_CHUNKS[m][1] * 2
        if m > 0:
            half_sent(m - 1)

        @pl.loop(0, 2)
        def _(h):
            multiply(m, 1 - c, half, h)
            half_copy(m, h).start()

        @pl.loop(0, 2)
        def _(h):
            multiply(m, c, own, h)

        @pl.loop(0, 2)
        def _(h):
            half_copy(m, h).wait_recv()
            for d in (2, 1, 3, 0):
                xd = (x + d) % NX
                r1[m, xd, :, h, :, :n] = r1[m, xd, :, h, :, :n] + own[xd, :, h, :, :n]
                for b in range(2):
                    dy = (h * 2 + b - y + NY) % NY
                    if d > 0:
                        xy_copy(m, d * NY + dy).start()
                    else:
                        @pl.when(dy > 0)
                        def _():
                            xy_copy(m, dy).start()

    def plane_stage(m):
        n = A_CHUNKS[m][1]

        @pl.loop(1, NX * NY)
        def _(off):
            xy_copy(m, off).wait_recv()

        total = r1[m, x, ylo, yhi, :, :2 * n]
        for off in range(1, NX * NY):
            total = total + xyr[m, off - 1, :, :2 * n]
        total = total.reshape(4 * n, 256)
        for zd in range(NZ):
            zb[m, zd, :n] = jnp.concatenate(
                [total[n * q:n * q + n, 32 * zd:32 * zd + 32] for q in range(4)], axis=1)

        @pl.loop(0, NZ - 1)
        def _(j):
            zr_copy(m, j).start()

    def last_stage(m):
        n = A_CHUNKS[m][1]

        @pl.loop(0, NZ - 1)
        def _(j):
            zr_copy(m, j).wait_recv()

        final = zb[m, z, :n]
        for d in range(1, NZ):
            final = final + zr[m, d - 1, :n]
        return final

    def y_sent(i):
        for h in range(2):
            @pl.loop(0, NZ)
            def _(zd):
                y_copy(i, h, zd).wait_send()

    def pass_sent(i):
        @pl.loop(0, 4)
        def _(j):
            for role in range(2):
                for cc in range(NC):
                    pass_copy(i, role, j, cc).wait_send()

    def xy_sent(m):
        @pl.loop(1, NX * NY)
        def _(off):
            xy_copy(m, off).wait_send()

    def zr_sent(m):
        @pl.loop(0, NZ - 1)
        def _(j):
            zr_copy(m, j).wait_send()

    def half_sent(m):
        for h in range(2):
            half_copy(m, h).wait_send()

    def denominators():
        lane = lax.broadcasted_iota(jnp.int32, (32, SLAB), 1)
        line = lax.broadcasted_iota(jnp.int32, (32, SLAB), 0)
        wanted = lane == (col % 4) * 32 + line
        slab_col = jnp.sum(jnp.where(wanted, slab_v[...], 0.0), axis=1, keepdims=True)
        which = lax.broadcasted_iota(jnp.int32, (1, JWIN), 1) == col // 4
        pair_col = jnp.sum(jnp.where(which, pair_v[...], 0.0), axis=1, keepdims=True)
        return vir_v[...] + (slab_col - pair_col)

    for h in range(2):
        first_load(h).start()
    barrier = pltpu.get_barrier_semaphore()
    for off in range(1, NX * NY):
        peer = device((x + off // NY) % NX, (y + off % NY) % NY, z, c)
        pl.semaphore_signal(barrier, inc=1, device_id=peer, device_id_type=MESH)
    for d in range(1, NZ):
        for cd in range(NC):
            pl.semaphore_signal(barrier, inc=1, device_id=device(x, y, (z + d) % NZ, cd), device_id_type=MESH)
    pl.semaphore_signal(barrier, inc=1, device_id=device(x, y, z, 1 - c), device_id_type=MESH)
    load(1).start()
    small_loads = [
        pltpu.make_async_copy(src, dst, small_sem.at[i])
        for i, (src, dst) in enumerate(((residual, res_v), (vir, vir_v), (slab, slab_v), (pair, pair_v)))]
    for cp in small_loads:
        cp.start()
    perm[...] = permutation(16)
    perm3[...] = permutation(8)

    prepare(0)
    prepare(1)
    forward(0)
    prepare(2)
    forward(1)
    prepare(3)
    arrived(0, pass_copy)
    sent(0)
    forward(2)
    prepare(4)
    arrived(1, pass_copy)
    sent(1)
    forward(3)
    prepare(5)
    complete(0)
    complete(1)
    arrived(2)
    sent(2)
    forward(4)
    pair_stage(0)
    arrived(3)
    sent(3)
    forward(5)
    pair_stage(1)
    plane_stage(0)
    for i in range(nw + na):
        y_sent(i)
    for i in range(nw):
        pass_sent(i)
    arrived(4)
    pair_stage(2)
    plane_stage(1)
    xy_sent(0)
    xy_sent(1)
    zr_sent(0)
    sent(4)
    arrived(5)
    pair_stage(3)
    plane_stage(2)
    for cp in small_loads:
        cp.wait()
    denom = denominators()
    finals = [last_stage(0), last_stage(1)]
    zr_sent(1)
    sent(5)
    half_sent(3)
    xy_sent(2)
    plane_stage(3)
    finals.append(last_stage(2))
    zr_sent(2)
    xy_sent(3)
    finals.append(last_stage(3))
    cycle = jnp.concatenate(
        [finals[m][:, 32 * q:32 * q + 32] for q in range(4) for m in range(na)], axis=0).T
    out[...] = (res_v[...] + cycle) / denom
    zr_sent(3)


def body(ampl, integrals, residual_in, vir_energy, slab_energy, pair_energy):
    DMA = pltpu.SemaphoreType.DMA
    nw, na = len(W_CHUNKS), len(A_CHUNKS)
    update = pl.pallas_call(
        kernel,
        out_shape=jax.ShapeDtypeStruct((32, 224), F32),
        in_specs=[pl.BlockSpec(memory_space=pl.ANY)] * 6,
        out_specs=pl.BlockSpec(memory_space=pltpu.VMEM),
        scratch_shapes=[
            pltpu.VMEM((2, 16, 32, C), BF),
            pltpu.VMEM((8, 32, C), BF),
            pltpu.VMEM((256, 256), BF),
            pltpu.VMEM((128, 128), BF),
            pltpu.VMEM((nw, 32, 16, C), BF),
            pltpu.VMEM((na - 1, 32, 16, C), BF),
            pltpu.VMEM((32, 8, C), BF),
            pltpu.VMEM((nw, 2, ZC, 16, C), BF),
            pltpu.VMEM((na - 1, 2, ZC, 16, C), BF),
            pltpu.VMEM((2, ZC, 8, C), BF),
            pltpu.VMEM((2, NC, 2, NZ, 32, C), BF),
            pltpu.VMEM((na - 1, 2, 4, 2, NC, 16, C), BF),
            pltpu.VMEM((2, 4, 2, NC, 8, C), BF),
            pltpu.VMEM((NX, 2, 2, 2, 32, 256), F32),
            pltpu.VMEM((NX, 2, 2, 2, 32, 256), F32),
            pltpu.VMEM((na, NX, 2, 2, 2, 32, 256), F32),
            pltpu.VMEM((na, NX * NY - 1, 2, 32, 256), F32),
            pltpu.VMEM((na, NZ, 16, 128), F32),
            pltpu.VMEM((na, NZ - 1, 16, 128), F32),
            pltpu.VMEM((32, 224), F32),
            pltpu.VMEM((1, 224), F32),
            pltpu.VMEM((1, SLAB), F32),
            pltpu.VMEM((1, JWIN), F32),
            DMA((2,)), DMA((2,)), DMA((4,)),
            DMA((nw + na, 2, NZ)), DMA((nw + na, 2, NZ)),
            DMA((nw + na, 2, 4, NC)), DMA((nw + na, 2, 4, NC)),
            DMA((nw, 2, 4, NC)), DMA((nw, 2, 4, NC)),
            DMA((nw + na, 2)),
            DMA((na, 2)), DMA((na, 2)),
            DMA((na, NX * NY - 1)), DMA((na, NX * NY - 1)),
            DMA((na, NZ - 1)), DMA((na, NZ - 1)),
        ],
        compiler_params=pltpu.CompilerParams(
            collective_id=0, has_side_effects=True, vmem_limit_bytes=60 * 1024 * 1024),
        cost_estimate=pl.CostEstimate(flops=2 * 1792 * 1024 * 1792, bytes_accessed=10 * 1024 * 1024, transcendentals=0),
        name="cycle",
    )(ampl, integrals, residual_in.T, vir_energy[None, :], slab_energy[None, :], pair_energy[None, :])
    return update.T


def solution(mesh):
    in_specs = (P("col", "row", None), P("col", "row", None), P("row", "col"), P("row"), P(), P())
    return jax.shard_map(body, mesh=mesh, in_specs=in_specs, out_specs=P("row", "col"), check_vma=False)
```

```python
import functools

import jax
import jax.numpy as jnp
from jax import lax
from jax.experimental import pallas as pl
from jax.experimental.pallas import tpu as pltpu
from jax.sharding import PartitionSpec as P

SLAB = 128
JWIN = 8
MESH = pl.DeviceIdType.MESH
BF = jnp.bfloat16
F32 = jnp.float32
NX, NY, NZ, NC = 4, 4, 8, 2
ZC = NZ * NC
C = 1792
A_CHUNKS = ((0, 16), (16, 16), (32, 16), (48, 8))
W_CHUNKS = ((0, 16), (16, 16))


def device(x, y, z, c):
    return ((y % 2) * NX + x, ((y // 2) * NZ + z) * NC + c)


def far_first(j):
    return jnp.where(j == NZ - 1, 0, jnp.where(j % 2 == 1, 4 - (j + 1) // 2, 4 + j // 2))


def need_order(t):
    return jnp.where(t % 2 == 0, 3 - t // 2, 4 + t // 2)


def permutation(rows):
    n = rows * 16
    bits = rows.bit_length() - 1
    out = lax.broadcasted_iota(jnp.int32, (n, n), 0)
    inp = lax.broadcasted_iota(jnp.int32, (n, n), 1)
    hit = ((out >> bits) == (inp & 15)) & ((out & (rows - 1)) == (inp >> 4))
    return jnp.where(hit, 1.0, 0.0).astype(BF)


def kernel(ampl, integ, residual, vir, slab, pair, out, xbuf, x3buf, perm, perm3, sw, sa, sa3, yw, ya, ya3, rw, ra, ra3,
           half, own, r1, xyr, zb, zr, res_v, vir_v, slab_v, pair_v,
           load_sem, first_sem, small_sem, ys, yrv, zs, zrv, ws, wrv, loc_sem, s0s, s0r, s1s, s1r, s3s, s3r):
    row = lax.axis_index("row")
    col = lax.axis_index("col")
    ylo, x = row // NX, row % NX
    yhi, z, c = col // ZC, (col // NC) % NZ, col % NC
    y = yhi * 2 + ylo
    zc = z * NC + c

    chunks = [(integ, s, n, sw.at[i], yw.at[i]) for i, (s, n) in enumerate(W_CHUNKS)]
    chunks += [(ampl, s, n, sa.at[i], ya.at[i]) for i, (s, n) in enumerate(A_CHUNKS[:-1])]
    chunks += [(ampl, *A_CHUNKS[-1], sa3, ya3)]
    nw, na = len(W_CHUNKS), len(A_CHUNKS)

    def load(i):
        src, start, rows, _, _ = chunks[i]
        dst = xbuf.at[i % 2] if rows == 16 else x3buf
        return pltpu.make_async_copy(src.at[pl.ds(start, rows)], dst, load_sem.at[i % 2])

    def first_load(h):
        ks = pl.ds(16 * h, 16)
        return pltpu.make_async_copy(integ.at[pl.ds(0, 16), ks], xbuf.at[0, :, ks], first_sem.at[h])

    def relayout(i, h):
        _, _, rows, send, _ = chunks[i]

        @pl.loop(0, C // 256)
        def _(j):
            lanes = pl.ds(pl.multiple_of(j * 256, 256), 256)
            if rows == 16:
                block = xbuf[i % 2, :, 16 * h:16 * h + 16, lanes].reshape(256, 256)
                moved = jnp.dot(perm[...], block, preferred_element_type=F32)
                send[16 * h:16 * h + 16, :, lanes] = moved.astype(BF).reshape(16, 16, 256)
            else:
                block = x3buf[:, 16 * h:16 * h + 16, lanes].reshape(128, 256)
                moved = jnp.dot(perm3[...], block, preferred_element_type=F32)
                send[16 * h:16 * h + 16, :, lanes] = moved.reshape(16, rows, 256).astype(BF)

    def y_copy(i, h, zd):
        _, _, _, send, recv = chunks[i]
        return pltpu.make_async_remote_copy(
            src_ref=send.at[pl.ds(h * ZC + zd * NC, NC)],
            dst_ref=recv.at[yhi, pl.ds(zd * NC, NC)],
            send_sem=ys.at[i, h, zd],
            recv_sem=yrv.at[i, yhi, zd],
            device_id=device(x, h * 2 + 1 - ylo, z, c),
            device_id_type=MESH,
        )

    def y_arrived(i, h, zd):
        _, _, _, send, recv = chunks[i]
        return pltpu.make_async_copy(
            send.at[pl.ds(h * ZC + zd * NC, NC)], recv.at[h, pl.ds(zd * NC, NC)], yrv.at[i, h, zd])

    def source(role, j):
        return (z - j if role == 0 else z + j) % NZ

    def slot(i, role, j, zz, cc):
        if i < nw:
            return rw.at[role, cc, :, zz, pl.ds(W_CHUNKS[i][0], 16)]
        if i < nw + na - 1:
            return ra.at[i - nw, role, j, :, cc]
        return ra3.at[role, j, :, cc]

    def z_copy(i, role, j, cd):
        zd = (z + j if role == 0 else z - j) % NZ
        kk = (zd - role) % NZ * NC + cd
        return pltpu.make_async_remote_copy(
            src_ref=chunks[i][4].at[:, kk],
            dst_ref=slot(i, role, j, z, c),
            send_sem=zs.at[i, role, j, cd],
            recv_sem=zrv.at[i, role, j, c],
            device_id=device(x, y, zd, cd),
            device_id_type=MESH,
        )

    def z_arrived(i, role, j, cc):
        dst = slot(i, role, j, source(role, j), cc)
        return pltpu.make_async_copy(chunks[i][4].at[:, cc], dst, zrv.at[i, role, j, cc])

    def own_copy(i, role):
        kk = (z - role) % NZ * NC + c
        return pltpu.make_async_copy(chunks[i][4].at[:, kk], slot(i, role, 0, z, c), loc_sem.at[i, role])

    def pass_copy(i, role, j, cc):
        ref = slot(i, role, j, source(role, j), cc)
        dst = slot(i, 1 - role, j, source(role, j), cc)
        return pltpu.make_async_remote_copy(
            src_ref=ref, dst_ref=dst,
            send_sem=ws.at[i, role, j, cc], recv_sem=wrv.at[i, 1 - role, j, cc],
            device_id=device(x, y, (z + 1 - 2 * role) % NZ, c), device_id_type=MESH)

    def passed(i, role, j, cc):
        zz = (z - 1 - j if role == 1 else z + 1 + j) % NZ
        dst = slot(i, role, j, zz, cc)
        return pltpu.make_async_copy(chunks[i][4].at[:, cc], dst, wrv.at[i, role, j, cc])

    def prepare(i):
        if i > 0:
            load(i).wait()
        for h in range(2):
            if i == 0:
                first_load(h).wait()
            relayout(i, h)
            if i == 0 and h == 0:
                pl.semaphore_wait(barrier, NX * NY - 1 + (NZ - 1) * NC + 1)

            @pl.loop(0, NZ)
            def _(j):
                y_copy(i, h, (z + need_order(j)) % NZ).start()

        if i + 2 < nw + na:
            load(i + 2).start()

    def forward(i):
        @pl.loop(0, 3)
        def _(t):
            j = 3 - t
            for role in range(2):
                kz = (z + j if role == 0 else z - j - 1) % NZ
                for h in range(2):
                    y_arrived(i, h, kz).wait()
                for cd in range(NC):
                    z_copy(i, role, j, cd).start()

        for role in range(2):
            for h in range(2):
                y_arrived(i, h, (z - role) % NZ).wait()
            z_copy(i, role, 0, 1 - c).start()
            own_copy(i, role).start()

    def sent(i):
        @pl.loop(1, 4)
        def _(j):
            for role in range(2):
                for cd in range(NC):
                    z_copy(i, role, j, cd).wait_send()

        for role in range(2):
            z_copy(i, role, 0, 1 - c).wait_send()

    def arrived(i, then=None):
        for role in range(2):
            z_arrived(i, role, 0, 1 - c).wait()
            own_copy(i, role).wait()
            if then is not None:
                for cc in range(NC):
                    then(i, role, 0, cc).start()

        @pl.loop(1, 4)
        def _(j):
            for role in range(2):
                for cc in range(NC):
                    z_arrived(i, role, j, cc).wait()
                    if then is not None:
                        then(i, role, j, cc).start()

    def complete(i):
        @pl.loop(0, 4)
        def _(j):
            for role in range(2):
                for cc in range(NC):
                    passed(i, role, j, cc).wait()

    contract = (((1,), (1,)), ((), ()))

    def multiply(m, cn, dst, h):
        rows = A_CHUNKS[m][1]
        n = rows * 2

        parts = []
        for role in range(2):
            if rows == 16:
                left = ra[m, role].reshape(256, C)
            else:
                left = ra3[role].astype(F32).reshape(rows * 16, C).astype(BF)
            part = lax.dot_general(
                left, rw[role, cn, h].reshape(256, C), contract, preferred_element_type=F32)
            parts.append(part.reshape(4, 2, n, 256))
        for role in range(2):
            for j in range(1, 4):
                zz = source(role, j)
                dst[zz // 2, :, h, zz % 2, :n, :] = parts[role][j]
        dst[z // 2, :, h, z % 2, :n, :] = parts[0][0] + parts[1][0]
        zz = (z + 4) % NZ
        dst[zz // 2, :, h, zz % 2, :n, :] = jnp.zeros((2, n, 256), F32)

    def half_copy(m, h):
        n = A_CHUNKS[m][1] * 2
        return pltpu.make_async_remote_copy(
            src_ref=half.at[:, :, h, :, pl.ds(0, n)], dst_ref=r1.at[m, :, :, h, :, pl.ds(0, n)],
            send_sem=s0s.at[m, h], recv_sem=s0r.at[m, h],
            device_id=device(x, y, z, 1 - c), device_id_type=MESH)

    def xy_copy(m, off):
        n = A_CHUNKS[m][1] * 2
        xd, yd = (x + off // NY) % NX, (y + off % NY) % NY
        return pltpu.make_async_remote_copy(
            src_ref=r1.at[m, xd, yd % 2, yd // 2, :, pl.ds(0, n)], dst_ref=xyr.at[m, off - 1, :, pl.ds(0, n)],
            send_sem=s1s.at[m, off - 1], recv_sem=s1r.at[m, off - 1],
            device_id=device(xd, yd, z, c), device_id_type=MESH)

    def zr_copy(m, j):
        n = A_CHUNKS[m][1]
        off = far_first(j)
        zd = (z + off) % NZ
        return pltpu.make_async_remote_copy(
            src_ref=zb.at[m, zd, pl.ds(0, n)], dst_ref=zr.at[m, off - 1, pl.ds(0, n)],
            send_sem=s3s.at[m, off - 1], recv_sem=s3r.at[m, off - 1],
            device_id=device(x, y, zd, c), device_id_type=MESH)

    def pair_stage(m):
        n = A_CHUNKS[m][1] * 2
        if m > 0:
            half_sent(m - 1)

        @pl.loop(0, 2)
        def _(h):
            multiply(m, 1 - c, half, h)
            half_copy(m, h).start()

        @pl.loop(0, 2)
        def _(h):
            multiply(m, c, own, h)

        @pl.loop(0, 2)
        def _(h):
            half_copy(m, h).wait_recv()
            for d in (2, 1, 3, 0):
                xd = (x + d) % NX
                r1[m, xd, :, h, :, :n] = r1[m, xd, :, h, :, :n] + own[xd, :, h, :, :n]
                for b in range(2):
                    dy = (h * 2 + b - y + NY) % NY
                    if d > 0:
                        xy_copy(m, d * NY + dy).start()
                    else:
                        @pl.when(dy > 0)
                        def _():
                            xy_copy(m, dy).start()

    def plane_stage(m):
        n = A_CHUNKS[m][1]

        @pl.loop(1, NX * NY)
        def _(off):
            xy_copy(m, off).wait_recv()

        total = r1[m, x, ylo, yhi, :, :2 * n]
        for off in range(1, NX * NY):
            total = total + xyr[m, off - 1, :, :2 * n]
        total = total.reshape(4 * n, 256)
        for zd in range(NZ):
            zb[m, zd, :n] = jnp.concatenate(
                [total[n * q:n * q + n, 32 * zd:32 * zd + 32] for q in range(4)], axis=1)

        @pl.loop(0, NZ - 1)
        def _(j):
            zr_copy(m, j).start()

    def last_stage(m):
        n = A_CHUNKS[m][1]

        @pl.loop(0, NZ - 1)
        def _(j):
            zr_copy(m, j).wait_recv()

        final = zb[m, z, :n]
        for d in range(1, NZ):
            final = final + zr[m, d - 1, :n]
        return final

    def y_sent(i):
        for h in range(2):
            @pl.loop(0, NZ)
            def _(zd):
                y_copy(i, h, zd).wait_send()

    def pass_sent(i):
        @pl.loop(0, 4)
        def _(j):
            for role in range(2):
                for cc in range(NC):
                    pass_copy(i, role, j, cc).wait_send()

    def xy_sent(m):
        @pl.loop(1, NX * NY)
        def _(off):
            xy_copy(m, off).wait_send()

    def zr_sent(m):
        @pl.loop(0, NZ - 1)
        def _(j):
            zr_copy(m, j).wait_send()

    def half_sent(m):
        for h in range(2):
            half_copy(m, h).wait_send()

    def denominators():
        lane = lax.broadcasted_iota(jnp.int32, (32, SLAB), 1)
        line = lax.broadcasted_iota(jnp.int32, (32, SLAB), 0)
        wanted = lane == (col % 4) * 32 + line
        slab_col = jnp.sum(jnp.where(wanted, slab_v[...], 0.0), axis=1, keepdims=True)
        which = lax.broadcasted_iota(jnp.int32, (1, JWIN), 1) == col // 4
        pair_col = jnp.sum(jnp.where(which, pair_v[...], 0.0), axis=1, keepdims=True)
        return vir_v[...] + (slab_col - pair_col)

    for h in range(2):
        first_load(h).start()
    barrier = pltpu.get_barrier_semaphore()
    for off in range(1, NX * NY):
        peer = device((x + off // NY) % NX, (y + off % NY) % NY, z, c)
        pl.semaphore_signal(barrier, inc=1, device_id=peer, device_id_type=MESH)
    for d in range(1, NZ):
        for cd in range(NC):
            pl.semaphore_signal(barrier, inc=1, device_id=device(x, y, (z + d) % NZ, cd), device_id_type=MESH)
    pl.semaphore_signal(barrier, inc=1, device_id=device(x, y, z, 1 - c), device_id_type=MESH)
    load(1).start()
    small_loads = [
        pltpu.make_async_copy(src, dst, small_sem.at[i])
        for i, (src, dst) in enumerate(((residual, res_v), (vir, vir_v), (slab, slab_v), (pair, pair_v)))]
    for cp in small_loads:
        cp.start()
    perm[...] = permutation(16)
    perm3[...] = permutation(8)

    prepare(0)
    prepare(1)
    forward(0)
    prepare(2)
    forward(1)
    prepare(3)
    arrived(0, pass_copy)
    sent(0)
    forward(2)
    prepare(4)
    arrived(1, pass_copy)
    sent(1)
    forward(3)
    prepare(5)
    complete(0)
    complete(1)
    arrived(2)
    sent(2)
    forward(4)
    pair_stage(0)
    arrived(3)
    sent(3)
    forward(5)
    pair_stage(1)
    plane_stage(0)
    for i in range(nw + na):
        y_sent(i)
    for i in range(nw):
        pass_sent(i)
    arrived(4)
    pair_stage(2)
    plane_stage(1)
    xy_sent(0)
    xy_sent(1)
    zr_sent(0)
    sent(4)
    arrived(5)
    pair_stage(3)
    plane_stage(2)
    for cp in small_loads:
        cp.wait()
    denom = denominators()
    finals = [last_stage(0), last_stage(1)]
    zr_sent(1)
    sent(5)
    half_sent(3)
    xy_sent(2)
    plane_stage(3)
    finals.append(last_stage(2))
    zr_sent(2)
    xy_sent(3)
    finals.append(last_stage(3))
    cycle = jnp.concatenate(
        [finals[m][:, 32 * q:32 * q + 32] for q in range(4) for m in range(na)], axis=0).T
    out[0] = res_v[...] + cycle
    out[1] = denom
    zr_sent(3)


def body(ampl, integrals, residual_in, vir_energy, slab_energy, pair_energy):
    DMA = pltpu.SemaphoreType.DMA
    nw, na = len(W_CHUNKS), len(A_CHUNKS)
    update = pl.pallas_call(
        kernel,
        out_shape=jax.ShapeDtypeStruct((2, 32, 224), F32),
        in_specs=[pl.BlockSpec(memory_space=pl.ANY)] * 6,
        out_specs=pl.BlockSpec(memory_space=pltpu.VMEM),
        scratch_shapes=[
            pltpu.VMEM((2, 16, 32, C), BF),
            pltpu.VMEM((8, 32, C), BF),
            pltpu.VMEM((256, 256), BF),
            pltpu.VMEM((128, 128), BF),
            pltpu.VMEM((nw, 32, 16, C), BF),
            pltpu.VMEM((na - 1, 32, 16, C), BF),
            pltpu.VMEM((32, 8, C), BF),
            pltpu.VMEM((nw, 2, ZC, 16, C), BF),
            pltpu.VMEM((na - 1, 2, ZC, 16, C), BF),
            pltpu.VMEM((2, ZC, 8, C), BF),
            pltpu.VMEM((2, NC, 2, NZ, 32, C), BF),
            pltpu.VMEM((na - 1, 2, 4, 2, NC, 16, C), BF),
            pltpu.VMEM((2, 4, 2, NC, 8, C), BF),
            pltpu.VMEM((NX, 2, 2, 2, 32, 256), F32),
            pltpu.VMEM((NX, 2, 2, 2, 32, 256), F32),
            pltpu.VMEM((na, NX, 2, 2, 2, 32, 256), F32),
            pltpu.VMEM((na, NX * NY - 1, 2, 32, 256), F32),
            pltpu.VMEM((na, NZ, 16, 128), F32),
            pltpu.VMEM((na, NZ - 1, 16, 128), F32),
            pltpu.VMEM((32, 224), F32),
            pltpu.VMEM((1, 224), F32),
            pltpu.VMEM((1, SLAB), F32),
            pltpu.VMEM((1, JWIN), F32),
            DMA((2,)), DMA((2,)), DMA((4,)),
            DMA((nw + na, 2, NZ)), DMA((nw + na, 2, NZ)),
            DMA((nw + na, 2, 4, NC)), DMA((nw + na, 2, 4, NC)),
            DMA((nw, 2, 4, NC)), DMA((nw, 2, 4, NC)),
            DMA((nw + na, 2)),
            DMA((na, 2)), DMA((na, 2)),
            DMA((na, NX * NY - 1)), DMA((na, NX * NY - 1)),
            DMA((na, NZ - 1)), DMA((na, NZ - 1)),
        ],
        compiler_params=pltpu.CompilerParams(
            collective_id=0, has_side_effects=True, vmem_limit_bytes=60 * 1024 * 1024),
        cost_estimate=pl.CostEstimate(flops=2 * 1792 * 1024 * 1792, bytes_accessed=10 * 1024 * 1024, transcendentals=0),
        name="cycle",
    )(ampl, integrals, residual_in.T, vir_energy[None, :], slab_energy[None, :], pair_energy[None, :])
    return (update[0] / update[1]).T


def solution(mesh):
    in_specs = (P("col", "row", None), P("col", "row", None), P("row", "col"), P("row"), P(), P())
    return jax.shard_map(body, mesh=mesh, in_specs=in_specs, out_specs=P("row", "col"), check_vma=False)
```

```python
import functools

import jax
import jax.numpy as jnp
from jax import lax
from jax.experimental import pallas as pl
from jax.experimental.pallas import tpu as pltpu
from jax.sharding import PartitionSpec as P

SLAB = 128
JWIN = 8
MESH = pl.DeviceIdType.MESH
BF = jnp.bfloat16
F32 = jnp.float32
NX, NY, NZ, NC = 4, 4, 8, 2
ZC = NZ * NC
C = 1792
A_CHUNKS = ((0, 16), (16, 16), (32, 16), (48, 8))
W_CHUNKS = ((0, 16), (16, 16))


def device(x, y, z, c):
    return ((y % 2) * NX + x, ((y // 2) * NZ + z) * NC + c)


def far_first(j):
    return jnp.where(j == NZ - 1, 0, jnp.where(j % 2 == 1, 4 - (j + 1) // 2, 4 + j // 2))


def need_order(t):
    return jnp.where(t % 2 == 0, 3 - t // 2, 4 + t // 2)


def permutation(rows):
    n = rows * 16
    bits = rows.bit_length() - 1
    out = lax.broadcasted_iota(jnp.int32, (n, n), 0)
    inp = lax.broadcasted_iota(jnp.int32, (n, n), 1)
    hit = ((out >> bits) == (inp & 15)) & ((out & (rows - 1)) == (inp >> 4))
    return jnp.where(hit, 1.0, 0.0).astype(BF)


def kernel(ampl, integ, residual, vir, slab, pair, out, xbuf, x3buf, perm, perm3, sw, sa, sa3, yw, ya, ya3, rw, ra, ra3,
           half, own, r1, xyr, zb, zr, res_v, vir_v, slab_v, pair_v,
           load_sem, first_sem, small_sem, ys, yrv, zs, zrv, ws, wrv, loc_sem, s0s, s0r, s1s, s1r, s3s, s3r):
    row = lax.axis_index("row")
    col = lax.axis_index("col")
    ylo, x = row // NX, row % NX
    yhi, z, c = col // ZC, (col // NC) % NZ, col % NC
    y = yhi * 2 + ylo
    zc = z * NC + c

    chunks = [(integ, s, n, sw.at[i], yw.at[i]) for i, (s, n) in enumerate(W_CHUNKS)]
    chunks += [(ampl, s, n, sa.at[i], ya.at[i]) for i, (s, n) in enumerate(A_CHUNKS[:-1])]
    chunks += [(ampl, *A_CHUNKS[-1], sa3, ya3)]
    nw, na = len(W_CHUNKS), len(A_CHUNKS)

    def load(i):
        src, start, rows, _, _ = chunks[i]
        dst = xbuf.at[i % 2] if rows == 16 else x3buf
        return pltpu.make_async_copy(src.at[pl.ds(start, rows)], dst, load_sem.at[i % 2])

    def first_load(h):
        ks = pl.ds(16 * h, 16)
        return pltpu.make_async_copy(integ.at[pl.ds(0, 16), ks], xbuf.at[0, :, ks], first_sem.at[h])

    def relayout(i, h):
        _, _, rows, send, _ = chunks[i]

        @pl.loop(0, C // 256)
        def _(j):
            lanes = pl.ds(pl.multiple_of(j * 256, 256), 256)
            if rows == 16:
                block = xbuf[i % 2, :, 16 * h:16 * h + 16, lanes].reshape(256, 256)
                moved = jnp.dot(perm[...], block, preferred_element_type=F32)
                send[16 * h:16 * h + 16, :, lanes] = moved.astype(BF).reshape(16, 16, 256)
            else:
                block = x3buf[:, 16 * h:16 * h + 16, lanes].reshape(128, 256)
                moved = jnp.dot(perm3[...], block, preferred_element_type=F32)
                send[16 * h:16 * h + 16, :, lanes] = moved.reshape(16, rows, 256).astype(BF)

    def y_copy(i, h, zd):
        _, _, _, send, recv = chunks[i]
        return pltpu.make_async_remote_copy(
            src_ref=send.at[pl.ds(h * ZC + zd * NC, NC)],
            dst_ref=recv.at[yhi, pl.ds(zd * NC, NC)],
            send_sem=ys.at[i, h, zd],
            recv_sem=yrv.at[i, yhi, zd],
            device_id=device(x, h * 2 + 1 - ylo, z, c),
            device_id_type=MESH,
        )

    def y_arrived(i, h, zd):
        _, _, _, send, recv = chunks[i]
        return pltpu.make_async_copy(
            send.at[pl.ds(h * ZC + zd * NC, NC)], recv.at[h, pl.ds(zd * NC, NC)], yrv.at[i, h, zd])

    def source(role, j):
        return (z - j if role == 0 else z + j) % NZ

    def slot(i, role, j, zz, cc):
        if i < nw:
            return rw.at[role, cc, :, zz, pl.ds(W_CHUNKS[i][0], 16)]
        if i < nw + na - 1:
            return ra.at[i - nw, role, j, :, cc]
        return ra3.at[role, j, :, cc]

    def z_copy(i, role, j, cd):
        zd = (z + j if role == 0 else z - j) % NZ
        kk = (zd - role) % NZ * NC + cd
        return pltpu.make_async_remote_copy(
            src_ref=chunks[i][4].at[:, kk],
            dst_ref=slot(i, role, j, z, c),
            send_sem=zs.at[i, role, j, cd],
            recv_sem=zrv.at[i, role, j, c],
            device_id=device(x, y, zd, cd),
            device_id_type=MESH,
        )

    def z_arrived(i, role, j, cc):
        dst = slot(i, role, j, source(role, j), cc)
        return pltpu.make_async_copy(chunks[i][4].at[:, cc], dst, zrv.at[i, role, j, cc])

    def own_copy(i, role):
        kk = (z - role) % NZ * NC + c
        return pltpu.make_async_copy(chunks[i][4].at[:, kk], slot(i, role, 0, z, c), loc_sem.at[i, role])

    def pass_copy(i, role, j, cc):
        ref = slot(i, role, j, source(role, j), cc)
        dst = slot(i, 1 - role, j, source(role, j), cc)
        return pltpu.make_async_remote_copy(
            src_ref=ref, dst_ref=dst,
            send_sem=ws.at[i, role, j, cc], recv_sem=wrv.at[i, 1 - role, j, cc],
            device_id=device(x, y, (z + 1 - 2 * role) % NZ, c), device_id_type=MESH)

    def passed(i, role, j, cc):
        zz = (z - 1 - j if role == 1 else z + 1 + j) % NZ
        dst = slot(i, role, j, zz, cc)
        return pltpu.make_async_copy(chunks[i][4].at[:, cc], dst, wrv.at[i, role, j, cc])

    def prepare(i):
        if i > 0:
            load(i).wait()
        for h in range(2):
            if i == 0:
                first_load(h).wait()
            relayout(i, h)
            if i == 0 and h == 0:
                pl.semaphore_wait(barrier, NX * NY - 1 + (NZ - 1) * NC + 1)

            @pl.loop(0, NZ)
            def _(j):
                y_copy(i, h, (z + need_order(j)) % NZ).start()

        if i + 2 < nw + na:
            load(i + 2).start()

    def forward(i):
        @pl.loop(0, 3)
        def _(t):
            j = 3 - t
            for role in range(2):
                kz = (z + j if role == 0 else z - j - 1) % NZ
                for h in range(2):
                    y_arrived(i, h, kz).wait()
                for cd in range(NC):
                    z_copy(i, role, j, cd).start()

        for role in range(2):
            for h in range(2):
                y_arrived(i, h, (z - role) % NZ).wait()
            z_copy(i, role, 0, 1 - c).start()
            own_copy(i, role).start()

    def sent(i):
        @pl.loop(1, 4)
        def _(j):
            for role in range(2):
                for cd in range(NC):
                    z_copy(i, role, j, cd).wait_send()

        for role in range(2):
            z_copy(i, role, 0, 1 - c).wait_send()

    def arrived(i, then=None):
        for role in range(2):
            z_arrived(i, role, 0, 1 - c).wait()
            own_copy(i, role).wait()
            if then is not None:
                for cc in range(NC):
                    then(i, role, 0, cc).start()

        @pl.loop(1, 4)
        def _(j):
            for role in range(2):
                for cc in range(NC):
                    z_arrived(i, role, j, cc).wait()
                    if then is not None:
                        then(i, role, j, cc).start()

    def complete(i):
        @pl.loop(0, 4)
        def _(j):
            for role in range(2):
                for cc in range(NC):
                    passed(i, role, j, cc).wait()

    contract = (((1,), (1,)), ((), ()))

    def multiply(m, cn, dst, h):
        rows = A_CHUNKS[m][1]
        n = rows * 2

        parts = []
        for role in range(2):
            if rows == 16:
                left = ra[m, role].reshape(256, C)
            else:
                left = ra3[role].astype(F32).reshape(rows * 16, C).astype(BF)
            part = lax.dot_general(
                left, rw[role, cn, h].reshape(256, C), contract, preferred_element_type=F32)
            parts.append(part.reshape(4, 2, n, 256))
        for role in range(2):
            for j in range(1, 4):
                zz = source(role, j)
                dst[zz // 2, :, h, zz % 2, :n, :] = parts[role][j]
        dst[z // 2, :, h, z % 2, :n, :] = parts[0][0] + parts[1][0]
        zz = (z + 4) % NZ
        dst[zz // 2, :, h, zz % 2, :n, :] = jnp.zeros((2, n, 256), F32)

    def half_copy(m, h):
        n = A_CHUNKS[m][1] * 2
        return pltpu.make_async_remote_copy(
            src_ref=half.at[:, :, h, :, pl.ds(0, n)], dst_ref=r1.at[m, :, :, h, :, pl.ds(0, n)],
            send_sem=s0s.at[m, h], recv_sem=s0r.at[m, h],
            device_id=device(x, y, z, 1 - c), device_id_type=MESH)

    def xy_copy(m, off):
        n = A_CHUNKS[m][1] * 2
        xd, yd = (x + off // NY) % NX, (y + off % NY) % NY
        return pltpu.make_async_remote_copy(
            src_ref=r1.at[m, xd, yd % 2, yd // 2, :, pl.ds(0, n)], dst_ref=xyr.at[m, off - 1, :, pl.ds(0, n)],
            send_sem=s1s.at[m, off - 1], recv_sem=s1r.at[m, off - 1],
            device_id=device(xd, yd, z, c), device_id_type=MESH)

    def zr_copy(m, j):
        n = A_CHUNKS[m][1]
        off = far_first(j)
        zd = (z + off) % NZ
        return pltpu.make_async_remote_copy(
            src_ref=zb.at[m, zd, pl.ds(0, n)], dst_ref=zr.at[m, off - 1, pl.ds(0, n)],
            send_sem=s3s.at[m, off - 1], recv_sem=s3r.at[m, off - 1],
            device_id=device(x, y, zd, c), device_id_type=MESH)

    def pair_stage(m):
        n = A_CHUNKS[m][1] * 2
        if m > 0:
            half_sent(m - 1)

        @pl.loop(0, 2)
        def _(h):
            multiply(m, 1 - c, half, h)
            half_copy(m, h).start()

        @pl.loop(0, 2)
        def _(h):
            multiply(m, c, own, h)
            half_copy(m, h).wait_recv()
            for d in (2, 1, 3, 0):
                xd = (x + d) % NX
                r1[m, xd, :, h, :, :n] = r1[m, xd, :, h, :, :n] + own[xd, :, h, :, :n]
                for b in range(2):
                    dy = (h * 2 + b - y + NY) % NY
                    if d > 0:
                        xy_copy(m, d * NY + dy).start()
                    else:
                        @pl.when(dy > 0)
                        def _():
                            xy_copy(m, dy).start()

    def plane_stage(m):
        n = A_CHUNKS[m][1]

        @pl.loop(1, NX * NY)
        def _(off):
            xy_copy(m, off).wait_recv()

        total = r1[m, x, ylo, yhi, :, :2 * n]
        for off in range(1, NX * NY):
            total = total + xyr[m, off - 1, :, :2 * n]
        total = total.reshape(4 * n, 256)
        for zd in range(NZ):
            zb[m, zd, :n] = jnp.concatenate(
                [total[n * q:n * q + n, 32 * zd:32 * zd + 32] for q in range(4)], axis=1)

        @pl.loop(0, NZ - 1)
        def _(j):
            zr_copy(m, j).start()

    def last_stage(m):
        n = A_CHUNKS[m][1]

        @pl.loop(0, NZ - 1)
        def _(j):
            zr_copy(m, j).wait_recv()

        final = zb[m, z, :n]
        for d in range(1, NZ):
            final = final + zr[m, d - 1, :n]
        return final

    def y_sent(i):
        for h in range(2):
            @pl.loop(0, NZ)
            def _(zd):
                y_copy(i, h, zd).wait_send()

    def pass_sent(i):
        @pl.loop(0, 4)
        def _(j):
            for role in range(2):
                for cc in range(NC):
                    pass_copy(i, role, j, cc).wait_send()

    def xy_sent(m):
        @pl.loop(1, NX * NY)
        def _(off):
            xy_copy(m, off).wait_send()

    def zr_sent(m):
        @pl.loop(0, NZ - 1)
        def _(j):
            zr_copy(m, j).wait_send()

    def half_sent(m):
        for h in range(2):
            half_copy(m, h).wait_send()

    def denominators():
        lane = lax.broadcasted_iota(jnp.int32, (32, SLAB), 1)
        line = lax.broadcasted_iota(jnp.int32, (32, SLAB), 0)
        wanted = lane == (col % 4) * 32 + line
        slab_col = jnp.sum(jnp.where(wanted, slab_v[...], 0.0), axis=1, keepdims=True)
        which = lax.broadcasted_iota(jnp.int32, (1, JWIN), 1) == col // 4
        pair_col = jnp.sum(jnp.where(which, pair_v[...], 0.0), axis=1, keepdims=True)
        return vir_v[...] + (slab_col - pair_col)

    for h in range(2):
        first_load(h).start()
    barrier = pltpu.get_barrier_semaphore()
    for off in range(1, NX * NY):
        peer = device((x + off // NY) % NX, (y + off % NY) % NY, z, c)
        pl.semaphore_signal(barrier, inc=1, device_id=peer, device_id_type=MESH)
    for d in range(1, NZ):
        for cd in range(NC):
            pl.semaphore_signal(barrier, inc=1, device_id=device(x, y, (z + d) % NZ, cd), device_id_type=MESH)
    pl.semaphore_signal(barrier, inc=1, device_id=device(x, y, z, 1 - c), device_id_type=MESH)
    load(1).start()
    small_loads = [
        pltpu.make_async_copy(src, dst, small_sem.at[i])
        for i, (src, dst) in enumerate(((residual, res_v), (vir, vir_v), (slab, slab_v), (pair, pair_v)))]
    for cp in small_loads:
        cp.start()
    perm[...] = permutation(16)
    perm3[...] = permutation(8)

    prepare(0)
    prepare(1)
    forward(0)
    prepare(2)
    forward(1)
    prepare(3)
    arrived(0, pass_copy)
    sent(0)
    forward(2)
    prepare(4)
    arrived(1, pass_copy)
    sent(1)
    forward(3)
    prepare(5)
    complete(0)
    complete(1)
    arrived(2)
    sent(2)
    forward(4)
    pair_stage(0)
    arrived(3)
    sent(3)
    forward(5)
    pair_stage(1)
    plane_stage(0)
    for i in range(nw + na):
        y_sent(i)
    for i in range(nw):
        pass_sent(i)
    arrived(4)
    pair_stage(2)
    plane_stage(1)
    xy_sent(0)
    xy_sent(1)
    zr_sent(0)
    sent(4)
    arrived(5)
    pair_stage(3)
    plane_stage(2)
    for cp in small_loads:
        cp.wait()
    denom = denominators()
    finals = [last_stage(0), last_stage(1)]
    zr_sent(1)
    sent(5)
    half_sent(3)
    xy_sent(2)
    plane_stage(3)
    finals.append(last_stage(2))
    zr_sent(2)
    xy_sent(3)
    finals.append(last_stage(3))
    cycle = jnp.concatenate(
        [finals[m][:, 32 * q:32 * q + 32] for q in range(4) for m in range(na)], axis=0).T
    out[...] = (res_v[...] + cycle) / denom
    zr_sent(3)


def body(ampl, integrals, residual_in, vir_energy, slab_energy, pair_energy):
    DMA = pltpu.SemaphoreType.DMA
    nw, na = len(W_CHUNKS), len(A_CHUNKS)
    update = pl.pallas_call(
        kernel,
        out_shape=jax.ShapeDtypeStruct((32, 224), F32),
        in_specs=[pl.BlockSpec(memory_space=pl.ANY)] * 6,
        out_specs=pl.BlockSpec(memory_space=pltpu.VMEM),
        scratch_shapes=[
            pltpu.VMEM((2, 16, 32, C), BF),
            pltpu.VMEM((8, 32, C), BF),
            pltpu.VMEM((256, 256), BF),
            pltpu.VMEM((128, 128), BF),
            pltpu.VMEM((nw, 32, 16, C), BF),
            pltpu.VMEM((na - 1, 32, 16, C), BF),
            pltpu.VMEM((32, 8, C), BF),
            pltpu.VMEM((nw, 2, ZC, 16, C), BF),
            pltpu.VMEM((na - 1, 2, ZC, 16, C), BF),
            pltpu.VMEM((2, ZC, 8, C), BF),
            pltpu.VMEM((2, NC, 2, NZ, 32, C), BF),
            pltpu.VMEM((na - 1, 2, 4, 2, NC, 16, C), BF),
            pltpu.VMEM((2, 4, 2, NC, 8, C), BF),
            pltpu.VMEM((NX, 2, 2, 2, 32, 256), F32),
            pltpu.VMEM((NX, 2, 2, 2, 32, 256), F32),
            pltpu.VMEM((na, NX, 2, 2, 2, 32, 256), F32),
            pltpu.VMEM((na, NX * NY - 1, 2, 32, 256), F32),
            pltpu.VMEM((na, NZ, 16, 128), F32),
            pltpu.VMEM((na, NZ - 1, 16, 128), F32),
            pltpu.VMEM((32, 224), F32),
            pltpu.VMEM((1, 224), F32),
            pltpu.VMEM((1, SLAB), F32),
            pltpu.VMEM((1, JWIN), F32),
            DMA((2,)), DMA((2,)), DMA((4,)),
            DMA((nw + na, 2, NZ)), DMA((nw + na, 2, NZ)),
            DMA((nw + na, 2, 4, NC)), DMA((nw + na, 2, 4, NC)),
            DMA((nw, 2, 4, NC)), DMA((nw, 2, 4, NC)),
            DMA((nw + na, 2)),
            DMA((na, 2)), DMA((na, 2)),
            DMA((na, NX * NY - 1)), DMA((na, NX * NY - 1)),
            DMA((na, NZ - 1)), DMA((na, NZ - 1)),
        ],
        compiler_params=pltpu.CompilerParams(
            collective_id=0, has_side_effects=True, vmem_limit_bytes=60 * 1024 * 1024),
        cost_estimate=pl.CostEstimate(flops=2 * 1792 * 1024 * 1792, bytes_accessed=10 * 1024 * 1024, transcendentals=0),
        name="cycle",
    )(ampl, integrals, residual_in.T, vir_energy[None, :], slab_energy[None, :], pair_energy[None, :])
    return update.T


def solution(mesh):
    in_specs = (P("col", "row", None), P("col", "row", None), P("row", "col"), P("row"), P(), P())
    return jax.shard_map(body, mesh=mesh, in_specs=in_specs, out_specs=P("row", "col"), check_vma=False)
```
